32 devices in a mesh: cfg: 2 (over core), blk: 4 (over z), req: 4 (over y, x).
Axes of the slice: x: 2, y: 2, z: 4, core: 2. Of those that a mesh axis runs over, the one named last changes fastest.
Arguments:
- residual: bfloat16 [2, 16, 2048], P('cfg'), may hold values from -6 to 6
- queries: bfloat16 [2, 16, 4096], P('cfg', 'req'), may hold values from -80 to 80
- new_entries: bfloat16 [2, 16, 2, 2048], P('cfg', 'req'), may hold values from -6 to 6
- key_cache: bfloat16 [2, 16, 192, 2048], P('cfg', 'req', 'blk'), may hold values from -6 to 6
- value_cache: bfloat16 [2, 16, 192, 2048], P('cfg', 'req', 'blk'), may hold values from -8 to 8
- lengths: int32 [2, 16], P('cfg', 'req'), may hold values from 2 to 192, as said below
- attention_ids: int32 [16, 2], replicated, may hold values from 0 to 7, all different within a row
- expert_ids: int32 [16, 2], replicated, may hold values from 0 to 7, all different within a row
- attention_router: bfloat16 [2048, 8], replicated, may hold values from -0.125 to 0.125
- expert_router: bfloat16 [2048, 8], replicated, may hold values from -0.125 to 0.125
- attention_output: bfloat16 [16384, 2048], P(('blk', 'req')), may hold values from -0.125 to 0.125
- expert_gain: bfloat16 [2048], replicated, may hold values from 0.25 to 1.75
- expert_gate: bfloat16 [45056, 2048], P(('blk', 'req')), may hold values from -0.125 to 0.125
- expert_up: bfloat16 [45056, 2048], P(('blk', 'req')), may hold values from -0.125 to 0.125
- expert_down: bfloat16 [45056, 2048], P(('blk', 'req')), may hold values from -0.078125 to 0.078125
- final_gain: bfloat16 [2048], replicated, may hold values from 0.25 to 1.75
- unembedding: bfloat16 [32000, 2048], P(('blk', 'req')), may hold values from -0.125 to 0.125
- tenant_sizes: int32 [4], replicated, may hold values from 1 to 8, 16 in all
- guidance: int32 [4], replicated, may hold values from 2 to 16
Outputs:
- guided: float32 [16, 32000], P('cfg', ('blk', 'req'))
The draws below stay inside these ranges and needn't reach their ends.
Inputs may be any that keep to these rules, and one draw needn't show every extreme that they name: lengths[0, i] lies from 96 to 192 and lengths[0, 0] = 192; lengths[1, i] lies from 2 to 48 and lengths[1, 0] = 48. `tenant_sizes`: the sizes sum to 16; the largest is exactly 8. `attention_ids`: the ids of one request differ. `expert_ids`: the ids of one request differ.
All inputs are finite; a program needn't handle non-finite values.
Results may differ from the reference program's by a relative error of at most 0.017.
Values may be sent and summed in bfloat16 or wider, within the bound.
A program may use at most 128 MiB of HBM per device.

```python
import math
import jax
import jax.numpy as jnp
import numpy as np
from jax import lax

D = 2048
H = 16
HD = 128
EA = 8
EM = 8
FF = 5632
V = 32000
TOPK = 2
TENANTS = 4
REQUESTS = 16
CAP = 192


def first_keys(key):
    sub_key = jax.random.fold_in(key, 101)
    shape = (2, REQUESTS, H, HD)
    return jnp.clip(jax.random.normal(sub_key, shape, jnp.float32), -6.0, 6.0)


def draw_key_cache(key, part):
    first = first_keys(key)
    second_key = jax.random.fold_in(key, 102)
    rest_key = jax.random.fold_in(key, 103)
    rest_shape = (2, REQUESTS, CAP - 2, H, HD)
    second = jnp.clip(jax.random.normal(second_key, first.shape, jnp.float32), -6.0, 6.0)
    rest = jnp.clip(jax.random.normal(rest_key, rest_shape, jnp.float32), -6.0, 6.0)
    whole = jnp.concatenate([first[:, :, None], second[:, :, None], rest], axis=2)
    return whole.reshape(2, REQUESTS, CAP, H * HD).astype(jnp.bfloat16)


def draw_value_cache(key, part):
    noise_key = jax.random.fold_in(key, 111)
    offset_key = jax.random.fold_in(key, 112)
    shape = (2, REQUESTS, CAP, H * HD)
    place = jnp.arange(CAP).astype(jnp.float32) / CAP
    noise = jnp.clip(jax.random.normal(noise_key, shape, jnp.float32), -5.0, 5.0)
    offset = jax.random.uniform(offset_key, (2, REQUESTS, 1, H * HD), jnp.float32, -1.5, 1.5)
    ramp = 0.5 + 1.5 * place
    whole = noise + offset * ramp[None, None, :, None]
    return whole.astype(jnp.bfloat16)


def draw_queries(key, part):
    sub_key = jax.random.fold_in(key, 105)
    whole = jnp.clip(jax.random.normal(sub_key, (2, REQUESTS, TOPK, H, HD), jnp.float32), -5.0, 5.0)
    return whole.reshape(2, REQUESTS, TOPK * H * HD).astype(jnp.bfloat16)


def draw_lengths(key, part):
    cond_key = jax.random.fold_in(key, 106)
    uncond_key = jax.random.fold_in(key, 107)
    conditional = jax.random.randint(cond_key, (REQUESTS,), CAP // 2, CAP + 1).astype(jnp.int32)
    conditional = conditional.at[0].set(CAP)
    unconditional = jax.random.randint(uncond_key, (REQUESTS,), 2, CAP // 4 + 1).astype(jnp.int32)
    unconditional = unconditional.at[0].set(CAP // 4)
    return jnp.stack([conditional, unconditional]).astype(jnp.int32)


def touch_ends(array, stream_key, least, high):
    extent = array.shape
    spot = [jax.random.randint(jax.random.fold_in(stream_key, axis), (), 0, extent[axis]) for axis in range(len(extent))]
    array = array.at[tuple(spot)].set(least)
    longest = extent.index(max(extent))
    spot[longest] = (spot[longest] + 1) % extent[longest]
    return array.at[tuple(spot)].set(high)


def shard_levels(key, dims, shards, low, top_value):
    gain, own = 1.0, jax.random.fold_in(key, 6)
    for dim, shards_of in shards:
        draws = jnp.exp(jax.random.uniform(jax.random.fold_in(own, dim), (shards_of,), jnp.float32, low / len(shards), top_value / len(shards)))
        gain = gain * jnp.repeat(draws, dims[dim] // shards_of).reshape([-1 if axis == dim else 1 for axis in range(len(dims))])
    return gain


def picks_of(stream_key, rows, number_of, top, lift):
    order = jax.random.permutation(jax.random.fold_in(stream_key, 1), number_of)
    boost = order
    for power in range(3):
        boost = boost * boost // number_of
    boost = boost * lift // number_of
    tickets = jax.random.randint(jax.random.fold_in(stream_key, 2), (rows, number_of), 0, 4096) + boost
    holders = jax.random.permutation(jax.random.fold_in(stream_key, 3), rows)[jnp.arange(number_of) % rows]
    tickets = jnp.where(jnp.arange(rows)[:, None] == holders[None, :], 1 << 14, tickets)
    merit = tickets * number_of + jnp.arange(number_of)
    return lax.top_k(merit.astype(jnp.int32), top)[1].astype(jnp.int32)


def split_up(number_of, total, reach, slope):
    portions = [(1 << 20) // math.isqrt(rank ** slope) + 1 for rank in range(2, number_of + 1)]
    spare, counts = total - reach - (number_of - 1), [1] * (number_of - 1)
    while spare > 0:
        free = [i for i in range(number_of - 1) if counts[i] < reach]
        pool, budget = sum([portions[i] for i in free]), spare
        for i in free:
            more = min(reach - counts[i], max(1, budget * portions[i] // pool), spare)
            counts[i] = counts[i] + more
            spare = spare - more
    return np.array([reach] + counts)


def ragged_sizes(rng, amount, total, reach, lean):
    if amount == 2:
        one = jax.random.randint(rng, (), max(1, total - reach), min(reach, total - 1) + 1)
        return jnp.stack([one, total - one])
    sizes = jnp.asarray(split_up(amount, total, reach, lean), jnp.int32)
    twos = (amount - 1) // 2
    giver, receiver = sizes[1:1 + 2 * twos:2], sizes[2:2 + 2 * twos:2]
    margin = jnp.minimum(giver - 1, reach - receiver)
    passed = jax.random.randint(jax.random.fold_in(rng, 1), (twos,), 0, 1 << 20) % (margin + 1)
    sizes = sizes.at[1:1 + 2 * twos:2].set(giver - passed).at[2:2 + 2 * twos:2].set(receiver + passed)
    return sizes[jax.random.permutation(jax.random.fold_in(rng, 2), amount)]


def scatter_about(stream_key, extent, scale, most, split=(), dtype=jnp.bfloat16):
    values = jax.random.normal(stream_key, extent, jnp.float32) * scale
    if len(split) > 0:
        values = shard_levels(stream_key, extent, split, -0.22, 0.18) * values
    return jnp.clip(values, min=-most, max=most).astype(dtype)


def setup_inputs(seed: int = 0) -> dict:
    streams_of = jax.random.split(jax.random.key(seed), 20)
    residual = scatter_about(streams_of[0], (2, REQUESTS, D), 1.0, 6.0, ((0, 2),))
    queries = draw_queries(jax.random.fold_in(streams_of[19], 71), 0)
    new_entries = scatter_about(streams_of[2], (2, REQUESTS, 2, H * HD), 1.0, 6.0, ((0, 2), (1, 4)))
    key_cache = draw_key_cache(jax.random.fold_in(streams_of[19], 71), 0)
    value_cache = draw_value_cache(jax.random.fold_in(streams_of[19], 71), 0)
    lengths = draw_lengths(jax.random.fold_in(streams_of[19], 71), 0)
    attention_ids = picks_of(streams_of[6], REQUESTS, EA, TOPK, 2048)
    expert_ids = picks_of(streams_of[7], REQUESTS, EM, TOPK, 2048)
    attention_router = scatter_about(streams_of[8], (D, EA), D ** -0.5, 0.125)
    expert_router = scatter_about(streams_of[9], (D, EM), D ** -0.5, 0.125)
    attention_output = scatter_about(streams_of[10], (EA * H * HD, D), (H * HD) ** -0.5, 0.125, ((0, 16),))
    expert_gain = jnp.clip(1.0 + 0.15 * jax.random.normal(streams_of[11], (D,), jnp.float32), 0.25, 1.75).astype(jnp.bfloat16)
    expert_gate = scatter_about(streams_of[12], (EM * FF, D), D ** -0.5, 0.125, ((0, 16),))
    expert_up = scatter_about(streams_of[13], (EM * FF, D), D ** -0.5, 0.125, ((0, 16),))
    expert_down = scatter_about(streams_of[14], (EM * FF, D), FF ** -0.5, 0.078125, ((0, 16),))
    final_gain = jnp.clip(1.0 + 0.15 * jax.random.normal(streams_of[15], (D,), jnp.float32), 0.25, 1.75).astype(jnp.bfloat16)
    unembedding = scatter_about(streams_of[16], (V, D), D ** -0.5, 0.125, ((0, 16),))
    tenant_sizes = ragged_sizes(streams_of[17], TENANTS, REQUESTS, REQUESTS // 2, 2).astype(jnp.int32)
    guidance = touch_ends(jax.random.randint(streams_of[18], (TENANTS,), 2, 17), jax.random.fold_in(streams_of[18], 1), 2, 16).astype(jnp.int32)
    return {"residual": residual, "queries": queries, "new_entries": new_entries, "key_cache": key_cache, "value_cache": value_cache, "lengths": lengths, "attention_ids": attention_ids, "expert_ids": expert_ids, "attention_router": attention_router, "expert_router": expert_router, "attention_output": attention_output, "expert_gain": expert_gain, "expert_gate": expert_gate, "expert_up": expert_up, "expert_down": expert_down, "final_gain": final_gain, "unembedding": unembedding, "tenant_sizes": tenant_sizes, "guidance": guidance}


EPS = 1e-05

def rms_scale(values):
    return values * lax.rsqrt(lax.optimization_barrier(jnp.mean(values * values, axis=-1, keepdims=True)) + EPS)

def pair_gates(logits, chosen_ids):
    experts = jnp.arange(logits.shape[-1])
    picked = lax.optimization_barrier(jnp.sum(jnp.where(chosen_ids[:, :, None] == experts[None, None, :], logits[:, None, :], 0.0), axis=-1))
    first = jax.nn.sigmoid(picked[:, 0] - picked[:, 1])
    second = jax.nn.sigmoid(picked[:, 1] - picked[:, 0])
    return jnp.stack([first, second], axis=1)

def attend_one(operands):
    query_row, key_rows, value_rows, entries, length = operands
    factor = 1.0 / math.sqrt(HD)
    query_heads = query_row.reshape(TOPK, H, HD).astype(jnp.float32)
    key_heads = key_rows.reshape(CAP, H, HD).astype(jnp.float32)
    value_heads = value_rows.reshape(CAP, H, HD).astype(jnp.float32)
    new_key = entries[0].reshape(H, HD).astype(jnp.float32)
    new_value = entries[1].reshape(H, HD).astype(jnp.float32)
    scores = jnp.einsum('khd,phd->khp', query_heads, key_heads) * factor
    new_score = jnp.einsum('khd,hd->kh', query_heads, new_key) * factor
    live = (jnp.arange(CAP) < length)[None, None, :]
    masked = jnp.where(live, scores, -jnp.inf)
    highest = jnp.maximum(lax.optimization_barrier(jnp.max(masked, axis=-1)), new_score)
    weights = jnp.where(live, jnp.exp(masked - highest[:, :, None]), 0.0)
    new_weight = jnp.exp(new_score - highest)
    denominator = lax.optimization_barrier(jnp.sum(weights, axis=-1)) + new_weight
    rounded = lax.optimization_barrier(weights.astype(jnp.bfloat16)).astype(jnp.float32)
    new_rounded = lax.optimization_barrier(new_weight.astype(jnp.bfloat16)).astype(jnp.float32)
    numerator = jnp.einsum('khp,phd->khd', rounded, value_heads) + new_rounded[:, :, None] * new_value[None, :, :]
    return (numerator / denominator[:, :, None]).astype(jnp.bfloat16).reshape(TOPK, H * HD)

def reference(residual, queries, new_entries, key_cache, value_cache, lengths, attention_ids, expert_ids, attention_router, expert_router, attention_output, expert_gain, expert_gate, expert_up, expert_down, final_gain, unembedding, tenant_sizes, guidance):
    total_rows = 2 * REQUESTS
    attention_out = lax.map(attend_one, (queries.reshape(total_rows, TOPK * H * HD), key_cache.reshape(total_rows, CAP, H * HD), value_cache.reshape(total_rows, CAP, H * HD), new_entries.reshape(total_rows, 2, H * HD), lengths.reshape(total_rows)))
    inputs = residual.reshape(total_rows, D).astype(jnp.float32)
    normed_input = rms_scale(inputs).astype(jnp.bfloat16)
    attention_both = jnp.concatenate([attention_ids, attention_ids], axis=0)
    expert_both = jnp.concatenate([expert_ids, expert_ids], axis=0)
    attention_gates = pair_gates(jnp.dot(normed_input, attention_router, preferred_element_type=jnp.float32), attention_both)
    gated_out = (attention_gates[:, :, None] * attention_out.astype(jnp.float32)).astype(jnp.bfloat16)
    attention_onehot = (attention_both[:, :, None] == jnp.arange(EA)[None, None, :]).astype(jnp.float32)
    placed = jnp.einsum('rke,rkf->ref', attention_onehot, gated_out.astype(jnp.float32)).astype(jnp.bfloat16)
    attention_proj = jnp.dot(placed.reshape(total_rows, EA * H * HD), attention_output, preferred_element_type=jnp.float32)
    middle = inputs + attention_proj
    expert_input = (rms_scale(middle) * expert_gain.astype(jnp.float32)).astype(jnp.bfloat16)
    expert_gates = pair_gates(jnp.dot(expert_input, expert_router, preferred_element_type=jnp.float32), expert_both)
    expert_onehot = (expert_both[:, :, None] == jnp.arange(EM)[None, None, :]).astype(jnp.float32)
    expert_share = jnp.einsum('rke,rk->re', expert_onehot, expert_gates)
    spread = jnp.repeat(expert_share, FF, axis=1)
    gate_values = jnp.dot(expert_input, expert_gate.T, preferred_element_type=jnp.float32)
    up_values = jnp.dot(expert_input, expert_up.T, preferred_element_type=jnp.float32)
    expert_hidden = (jax.nn.silu(gate_values) * up_values * spread).astype(jnp.bfloat16)
    expert_out = jnp.dot(expert_hidden, expert_down, preferred_element_type=jnp.float32)
    final_input = (rms_scale(middle + expert_out) * final_gain.astype(jnp.float32)).astype(jnp.bfloat16)
    logits = jnp.dot(final_input, unembedding.T, preferred_element_type=jnp.float32).reshape(2, REQUESTS, V)
    request_index = jnp.arange(REQUESTS).astype(jnp.int32)
    tenant_ends = jnp.cumsum(tenant_sizes).astype(jnp.int32)
    tenant = lax.optimization_barrier(jnp.sum((request_index[:, None] >= tenant_ends[None, :]).astype(jnp.int32), axis=1))
    tenant_onehot = tenant[:, None] == jnp.arange(TENANTS)[None, :]
    factor = lax.optimization_barrier(jnp.sum(jnp.where(tenant_onehot, guidance[None, :], 0), axis=1)).astype(jnp.float32) / 4.0
    return logits[1] + factor[:, None] * (logits[0] - logits[1])
```

```python
import math

import jax
import jax.numpy as jnp
from jax import lax
from jax.experimental import pallas as pl
from jax.experimental.pallas import tpu as pltpu
from jax.sharding import PartitionSpec as P

H = 16
HD = 128
FF = 5632
TOPK = 2


EPS = 1e-05


def joined(shard, axis, combine):
    everything = jax.tree.map(
        lambda part, kind: lax.all_gather(part.astype(kind), axis),
        shard,
        (jnp.bfloat16, jnp.bfloat16, jnp.bfloat16),
    )

    def take(k):
        return jax.tree.map(lambda part, own: part[k].astype(own.dtype), everything, shard)

    return lax.fori_loop(
        1, lax.axis_size(axis), lambda k, so_far: combine(so_far, take(k)), take(0)
    )


def swapped(value, axis, bit):
    mask = 2**bit
    pairs = [(source, source ^ mask) for source in range(lax.axis_size(axis))]
    return lax.ppermute(value, axis, pairs)


def rms_scale(values):
    return values * lax.rsqrt(jnp.mean(values * values, axis=-1, keepdims=True) + EPS)


def pair_gates(logits, chosen_ids):
    experts = jnp.arange(logits.shape[-1])
    picked = jnp.sum(
        jnp.where(chosen_ids[:, :, None] == experts[None, None, :], logits[:, None, :], 0.0),
        axis=-1,
    )
    first = jax.nn.sigmoid(picked[:, 0] - picked[:, 1])
    second = jax.nn.sigmoid(picked[:, 1] - picked[:, 0])
    return jnp.stack([first, second], axis=1)


def merge_parts(first_part, second_part):
    top_first, sum_first, acc_first = first_part
    top_second, sum_second, acc_second = second_part
    highest = jnp.maximum(top_first, top_second)
    scale_first = jnp.exp(top_first - highest)
    scale_second = jnp.exp(top_second - highest)
    merged_sum = sum_first * scale_first + sum_second * scale_second
    merged_acc = acc_first * scale_first[..., None] + acc_second * scale_second[..., None]
    return (highest, merged_sum, merged_acc)


def local(
    residual,
    queries,
    new_entries,
    key_cache,
    value_cache,
    lengths,
    attention_ids,
    expert_ids,
    attention_router,
    expert_router,
    attention_output,
    expert_gain,
    expert_gate,
    expert_up,
    expert_down,
    final_gain,
    unembedding,
    tenant_sizes,
    guidance,
):
    factor_scale = 1.0 / math.sqrt(HD)
    slot_rows = queries.shape[1]
    positions_local = key_cache.shape[2]
    feature_width = H * HD
    blk_index = lax.axis_index("blk")
    linear_index = blk_index * lax.axis_size("req") + lax.axis_index("req")
    query_heads = queries[0].reshape(slot_rows, TOPK, H, HD)
    key_heads = key_cache[0].reshape(slot_rows, positions_local, H, HD)
    value_heads = value_cache[0].reshape(slot_rows, positions_local, H, HD)
    scores = (
        jnp.einsum("rkhd,rphd->rkhp", query_heads, key_heads, preferred_element_type=jnp.float32)
        * factor_scale
    )
    positions = blk_index * positions_local + jnp.arange(positions_local)
    live = (positions[None, :] < lengths[0][:, None])[:, None, None, :]
    local_top = jnp.max(jnp.where(live, scores, -1e30), axis=-1)
    weights_local = jnp.where(live, jnp.exp(scores - local_top[..., None]), 0.0)
    weight_sums = jnp.sum(weights_local, axis=-1)
    weighted = jnp.einsum(
        "rkhp,rphd->rkhd",
        weights_local.astype(jnp.bfloat16),
        value_heads,
        preferred_element_type=jnp.float32,
    )
    highest, weight_sums, weighted = joined((local_top, weight_sums, weighted), "blk", merge_parts)
    new_keys = new_entries[0][:, 0].reshape(slot_rows, H, HD)
    new_values = new_entries[0][:, 1].reshape(slot_rows, H, HD)
    new_score = (
        jnp.einsum("rkhd,rhd->rkh", query_heads, new_keys, preferred_element_type=jnp.float32)
        * factor_scale
    )
    peak = jnp.maximum(highest, new_score)
    shrink = jnp.exp(highest - peak)
    fresh = jnp.exp(new_score - peak)
    denominator = weight_sums * shrink + fresh
    fresh_rounded = fresh.astype(jnp.bfloat16)
    numerator = weighted * shrink[..., None] + jnp.einsum(
        "rkh,rhd->rkhd", fresh_rounded, new_values, preferred_element_type=jnp.float32
    )
    attention_out = (
        (numerator / denominator[..., None])
        .astype(jnp.bfloat16)
        .reshape(slot_rows, TOPK, feature_width)
    )
    inputs = residual[0].astype(jnp.float32)
    normed_input = rms_scale(inputs).astype(jnp.bfloat16)
    attention_gates = pair_gates(
        jnp.dot(normed_input, attention_router, preferred_element_type=jnp.float32), attention_ids
    )
    proj_rows = attention_output.shape[0]
    first_row = linear_index * proj_rows
    own_expert = first_row // feature_width
    own_column = first_row % feature_width
    picked = (attention_ids == own_expert).astype(jnp.float32) * attention_gates
    columns = lax.dynamic_slice_in_dim(
        lax.all_gather(attention_out, "req", axis=0, tiled=True), own_column, proj_rows, 2
    ).astype(jnp.float32)
    selected = jnp.sum(picked[:, :, None] * columns, axis=1).astype(jnp.bfloat16)
    proj_terms = jnp.dot(selected, attention_output, preferred_element_type=jnp.float32)
    attention_proj = lax.psum(proj_terms, ("blk", "req"))
    middle = inputs + attention_proj
    expert_input = (rms_scale(middle) * expert_gain.astype(jnp.float32)).astype(jnp.bfloat16)
    expert_gates = pair_gates(
        jnp.dot(expert_input, expert_router, preferred_element_type=jnp.float32), expert_ids
    )
    hidden_rows = expert_gate.shape[0]
    hidden_expert = linear_index * hidden_rows // FF
    expert_share = jnp.sum((expert_ids == hidden_expert).astype(jnp.float32) * expert_gates, axis=1)
    gate_values = jnp.einsum(
        "rd,fd->rf", expert_input, expert_gate, preferred_element_type=jnp.float32
    )
    up_values = jnp.einsum("rd,fd->rf", expert_input, expert_up, preferred_element_type=jnp.float32)
    expert_hidden = (jax.nn.silu(gate_values) * up_values * expert_share[:, None]).astype(
        jnp.bfloat16
    )
    expert_terms = jnp.dot(expert_hidden, expert_down, preferred_element_type=jnp.float32)
    expert_out = lax.psum(expert_terms, ("blk", "req"))
    final_input = (rms_scale(middle + expert_out) * final_gain.astype(jnp.float32)).astype(
        jnp.bfloat16
    )
    logits = jnp.einsum("rd,vd->rv", final_input, unembedding, preferred_element_type=jnp.float32)
    stream_index = lax.axis_index("cfg")
    half_rows = logits.shape[0] // 2
    own_rows = lax.dynamic_slice_in_dim(logits, stream_index * half_rows, half_rows, 0)
    other_rows = lax.dynamic_slice_in_dim(logits, (1 - stream_index) * half_rows, half_rows, 0)
    partner = swapped(other_rows, "cfg", 0)
    first_stream = stream_index == 0
    conditional = jnp.where(first_stream, own_rows, partner)
    unconditional = jnp.where(first_stream, partner, own_rows)
    request_index = stream_index * half_rows + jnp.arange(half_rows)
    tenant_ends = jnp.cumsum(tenant_sizes)
    tenant = jnp.sum((request_index[:, None] >= tenant_ends[None, :]).astype(jnp.int32), axis=1)
    tenant_onehot = tenant[:, None] == jnp.arange(tenant_sizes.shape[0])[None, :]
    factor = (
        jnp.sum(jnp.where(tenant_onehot, guidance[None, :], 0), axis=1).astype(jnp.float32) / 4.0
    )
    return unconditional + factor[:, None] * (conditional - unconditional)


LANES = 128
F32 = jnp.float32
BF16 = jnp.bfloat16
MESH = pl.DeviceIdType.MESH
DEAD = -1e30


def fits(mesh):
    shape = dict(mesh.shape)
    return shape["cfg"] == 2 and shape["blk"] == 4 and shape["req"] == 4


def dot_nt(left, right):
    return lax.dot_general(left, right, (((1,), (1,)), ((), ())), preferred_element_type=F32)


def kernel_gates(logits, ids):
    experts = lax.broadcasted_iota(jnp.int32, logits.shape, 1)
    first = jnp.sum(jnp.where(experts == ids[:, 0:1], logits, 0.0), axis=1, keepdims=True)
    second = jnp.sum(jnp.where(experts == ids[:, 1:2], logits, 0.0), axis=1, keepdims=True)
    return jax.nn.sigmoid(first - second), jax.nn.sigmoid(second - first)


def expert_share_of(logits, ids, expert):
    first, second = kernel_gates(logits, ids)
    return jnp.where(ids[:, 0:1] == expert, first, 0.0) + jnp.where(
        ids[:, 1:2] == expert, second, 0.0
    )


def step_kernel(
    n_blk,
    n_req,
    residual,
    queries,
    new_entries,
    key_cache,
    value_cache,
    lengths,
    att_ids,
    att_ids_s,
    exp_ids,
    att_router,
    exp_router,
    w_proj,
    gains,
    w_gate,
    w_up,
    w_down,
    w_head,
    sizes,
    guidance,
    out,
    keys,
    values,
    v_proj,
    v_gate,
    v_up,
    v_down,
    v_head,
    send_a,
    recv_a,
    joint,
    send_r,
    recv_r,
    send_g,
    recv_g,
    send_q,
    recv_q,
    send_f,
    recv_f,
    own_middle,
    hidden,
    kv_sem,
    w_sem,
    sems_s,
    sems_r,
    fin_s,
    fin_r,
):
    n = n_blk * n_req
    cfg = lax.axis_index("cfg")
    blk = lax.axis_index("blk")
    req = lax.axis_index("req")
    me = blk * n_req + req
    rows = queries.shape[1]
    local_pos = key_cache.shape[2]
    width = H * HD

    barrier = pltpu.get_barrier_semaphore()

    def greet(k, carry):
        other = lax.rem(me + k, n)
        for side in (0, 1):
            pl.semaphore_signal(
                barrier,
                inc=1,
                device_id=(side, other // n_req, lax.rem(other, n_req)),
                device_id_type=MESH,
            )
        return carry

    lax.fori_loop(1, n, greet, 0)
    pl.semaphore_signal(barrier, inc=1, device_id=(1 - cfg, blk, req), device_id_type=MESH)

    cache_copies = []
    for r in range(rows):
        for which, (source, target) in enumerate(((key_cache, keys), (value_cache, values))):
            copy = pltpu.make_async_copy(
                source.at[0, r], target.at[r, pl.ds(0, local_pos)], kv_sem.at[which, r]
            )
            copy.start()
            cache_copies.append(copy)
    weight_copies = []
    for source, target in (
        (w_proj, v_proj),
        (w_gate, v_gate),
        (w_up, v_up),
        (w_down, v_down),
        (w_head, v_head),
    ):
        copy = pltpu.make_async_copy(source, target, w_sem.at[len(weight_copies)])
        copy.start()
        weight_copies.append(copy)

    def send(source_of, target, phase, k):
        other = lax.rem(me + k, n)
        return pltpu.make_async_remote_copy(
            src_ref=source_of(other),
            dst_ref=target.at[me],
            send_sem=sems_s.at[phase, other],
            recv_sem=sems_r.at[phase, me],
            device_id=(cfg, other // n_req, lax.rem(other, n_req)),
            device_id_type=MESH,
        )

    def start_all(source_of, target, phase):
        def go(k, carry):
            send(source_of, target, phase, k).start()
            return carry

        lax.fori_loop(1, n, go, 0)

    def finish_all(source_of, target, phase):
        def go(k, carry):
            source = lax.rem(me + n - k, n)
            pltpu.make_async_remote_copy(
                src_ref=source_of(me),
                dst_ref=target.at[source],
                send_sem=sems_s.at[phase, source],
                recv_sem=sems_r.at[phase, source],
                device_id=(cfg, source // n_req, lax.rem(source, n_req)),
                device_id_type=MESH,
            ).wait()
            return carry

        lax.fori_loop(1, n, go, 0)

    extra = keys.shape[1] - local_pos
    head_of_row = lax.rem(lax.broadcasted_iota(jnp.int32, (TOPK * H, 1), 0), H)
    head_of_column = lax.broadcasted_iota(jnp.int32, (TOPK * H, width), 1) // HD
    own_head = head_of_row == head_of_column
    place = lax.broadcasted_iota(jnp.int32, (1, keys.shape[1]), 1)
    new_row = lax.broadcasted_iota(jnp.int32, (extra, 1), 0) == 0
    query_all = queries[0].astype(F32)
    outs = []
    tops = []
    for r in range(rows):
        entries = new_entries[0, r].astype(F32)
        keys[r, pl.ds(local_pos, extra)] = jnp.where(new_row, entries[0:1], 0.0).astype(BF16)
        values[r, pl.ds(local_pos, extra)] = jnp.where(new_row, entries[1:2], 0.0).astype(BF16)
        cache_copies[2 * r].wait()
        cache_copies[2 * r + 1].wait()
        spread = jnp.concatenate(
            [
                jnp.broadcast_to(query_all[r : r + 1, k * width : (k + 1) * width], (H, width))
                for k in range(TOPK)
            ],
            axis=0,
        )
        spread = jnp.where(own_head, spread, 0.0).astype(BF16)
        scores = dot_nt(spread, keys[r]) * (1.0 / math.sqrt(HD))
        cached = (place < local_pos) & (place + blk * local_pos < lengths[0, r])
        live = cached | ((place == local_pos) & (blk == 0))
        top = jnp.max(jnp.where(live, scores, DEAD), axis=1, keepdims=True)
        weights = jnp.where(live, jnp.exp(scores - top), 0.0)
        total = jnp.sum(weights, axis=1, keepdims=True)
        wide = jnp.dot(weights.astype(BF16), values[r], preferred_element_type=F32)
        acc = jnp.zeros((TOPK * H, HD), F32)
        for h in range(H):
            acc = acc + jnp.where(head_of_row == h, wide[:, h * HD : (h + 1) * HD], 0.0)
        alive = total > 0.0
        safe = jnp.where(alive, total, 1.0)
        outs.append(acc / safe)
        tops.append(jnp.where(alive, top + jnp.log(safe), DEAD))

    lane = lax.broadcasted_iota(jnp.int32, (2 * H, LANES), 1)
    half = H // 2
    for e in range(n // 2):
        picked = []
        levels = []
        for r in range(rows):
            first = jnp.where(att_ids_s[req * rows + r, 0] == e, 1.0, 0.0)
            second = jnp.where(att_ids_s[req * rows + r, 1] == e, 1.0, 0.0)
            picked.append(first * outs[r][:H] + second * outs[r][H:])
            levels.append(first * tops[r][:H] + second * tops[r][H:])
        for side in range(2):
            cut = slice(side * half, (side + 1) * half)
            block = jnp.concatenate([part[cut] for part in picked], axis=0)
            level = jnp.concatenate([part[cut] for part in levels], axis=0)
            high = level.astype(BF16).astype(F32)
            mid = (level - high).astype(BF16).astype(F32)
            low = level - high - mid
            parts = jnp.where(
                lax.rem(lane, 3) == 0, high, jnp.where(lax.rem(lane, 3) == 1, mid, low)
            )
            stats = jnp.where(
                lane[:H] < 3, parts[:H], jnp.where(lane[:H] < 6, parts[H:], 0.0)
            )
            send_a[2 * e + side] = jnp.concatenate([block, stats], axis=0).astype(BF16)

    pl.semaphore_wait(barrier, 2 * n - 1)
    start_all(lambda other: send_a.at[other], recv_a, 0)
    recv_a[me] = send_a[me]

    inputs = residual[0].astype(F32)
    normed = rms_scale(inputs).astype(BF16)
    att_logits = jnp.dot(normed, att_router[...], preferred_element_type=F32)
    att_share = expert_share_of(att_logits, att_ids[...], me // 2)
    weight_copies[0].wait()
    finish_all(lambda other: send_a.at[other], recv_a, 0)

    small = lax.broadcasted_iota(jnp.int32, (H, LANES), 1)
    for q in range(n_req):
        blocks = []
        levels = []
        for b in range(n_blk):
            message = recv_a[b * n_req + q].astype(F32)
            stats = message[2 * H :]
            upper = jnp.sum(jnp.where(small < 3, stats, 0.0), axis=1, keepdims=True)
            lower = jnp.sum(
                jnp.where((small >= 3) & (small < 6), stats, 0.0), axis=1, keepdims=True
            )
            levels.append(jnp.concatenate([upper, lower], axis=0))
            blocks.append(message[: 2 * H])
        peak = levels[0]
        for b in range(1, n_blk):
            peak = jnp.maximum(peak, levels[b])
        total = jnp.zeros_like(peak)
        mixed = jnp.zeros_like(blocks[0])
        for b in range(n_blk):
            weight = jnp.exp(levels[b] - peak)
            total = total + weight
            mixed = mixed + weight * blocks[b]
        joint[pl.ds(q * 2 * H, 2 * H)] = (mixed / total).astype(BF16).astype(F32)
    gathered = jnp.concatenate(
        [joint[pl.ds(h, n_req * rows, stride=half), :] for h in range(half)], axis=1
    )
    selected = (gathered * att_share).astype(BF16)

    def scatter(product_of, send_buf):
        for t in range(4):
            part = product_of(t)
            for j in range(4):
                send_buf[4 * t + j] = part[:, j * LANES : (j + 1) * LANES].astype(BF16)

    def summed(buf):
        total = buf[0].astype(F32)
        for k in range(1, n):
            total = total + buf[k].astype(F32)
        return total

    def whole(buf):
        return jnp.concatenate([buf[k].astype(F32) for k in range(n)], axis=1)

    scatter(
        lambda t: jnp.dot(
            selected, v_proj[:, t * 512 : (t + 1) * 512], preferred_element_type=F32
        ),
        send_r,
    )
    start_all(lambda other: send_r.at[other], recv_r, 1)
    recv_r[me] = send_r[me]
    finish_all(lambda other: send_r.at[other], recv_r, 1)
    own_column = pl.multiple_of(me * LANES, LANES)
    own_middle[...] = summed(recv_r) + residual[0, :, pl.ds(own_column, LANES)].astype(F32)
    send_g[...] = own_middle[...].astype(BF16)
    start_all(lambda other: send_g, recv_g, 2)
    recv_g[me] = send_g[...]
    weight_copies[1].wait()
    weight_copies[2].wait()
    finish_all(lambda other: send_g, recv_g, 2)

    expert_input = (rms_scale(whole(recv_g)) * gains[0:1, :]).astype(BF16)
    exp_logits = jnp.dot(expert_input, exp_router[...], preferred_element_type=F32)
    share = expert_share_of(exp_logits, exp_ids[...], me * v_gate.shape[0] // FF)

    def feed(t, carry):
        start = pl.multiple_of(t * 256, 256)
        gate_values = dot_nt(expert_input, v_gate[pl.ds(start, 256), :])
        up_values = dot_nt(expert_input, v_up[pl.ds(start, 256), :])
        hidden[t] = (jax.nn.silu(gate_values) * up_values * share).astype(BF16)
        return carry

    tiles = v_gate.shape[0] // 256
    lax.fori_loop(0, tiles, feed, 0)
    weight_copies[3].wait()
    all_hidden = jnp.concatenate([hidden[t] for t in range(tiles)], axis=1)
    scatter(
        lambda t: jnp.dot(
            all_hidden, v_down[:, t * 512 : (t + 1) * 512], preferred_element_type=F32
        ),
        send_q,
    )
    start_all(lambda other: send_q.at[other], recv_q, 3)
    recv_q[me] = send_q[me]
    finish_all(lambda other: send_q.at[other], recv_q, 3)
    send_f[...] = (own_middle[...] + summed(recv_q)).astype(BF16)

    def final_copy(k, side, other, source_side, source):
        return pltpu.make_async_remote_copy(
            src_ref=send_f,
            dst_ref=recv_f.at[source_side, source],
            send_sem=fin_s.at[lax.rem(side + 2 - source_side, 2), k],
            recv_sem=fin_r.at[source_side, source],
            device_id=(side, other // n_req, lax.rem(other, n_req)),
            device_id_type=MESH,
        )

    def final_send(k, carry):
        other = lax.rem(me + k, n)
        final_copy(k, cfg, other, cfg, me).start()
        final_copy(k, 1 - cfg, other, cfg, me).start()
        return carry

    def final_wait(k, carry):
        source = lax.rem(me + n - k, n)
        for side in (0, 1):
            pltpu.make_async_remote_copy(
                src_ref=send_f,
                dst_ref=recv_f.at[lax.rem(cfg + side, 2), source],
                send_sem=fin_s.at[side, k],
                recv_sem=fin_r.at[lax.rem(cfg + side, 2), source],
                device_id=(lax.rem(cfg + side, 2), source // n_req, lax.rem(source, n_req)),
                device_id_type=MESH,
            ).wait()
        return carry

    final_copy(0, 1 - cfg, me, cfg, me).start()
    lax.fori_loop(1, n, final_send, 0)
    recv_f[cfg, me] = send_f[...]
    weight_copies[4].wait()
    pltpu.make_async_remote_copy(
        src_ref=send_f,
        dst_ref=recv_f.at[1 - cfg, me],
        send_sem=fin_s.at[1, 0],
        recv_sem=fin_r.at[1 - cfg, me],
        device_id=(1 - cfg, blk, req),
        device_id_type=MESH,
    ).wait()
    lax.fori_loop(1, n, final_wait, 0)

    guided_rows = out.shape[0]
    mine = []
    for stream in (0, 1):
        both = whole(recv_f.at[stream])
        mine.append(jnp.where(cfg == 0, both[:guided_rows], both[guided_rows:]))
    final_input = (rms_scale(jnp.concatenate(mine, axis=0)) * gains[1:2, :]).astype(BF16)
    request = cfg * guided_rows + lax.broadcasted_iota(jnp.int32, (guided_rows, LANES), 0)
    tenant = jnp.zeros_like(request)
    end = 0
    for t in range(sizes.shape[0]):
        end = end + sizes[t]
        tenant = tenant + jnp.where(request >= end, 1, 0)
    guide = jnp.zeros_like(request)
    for t in range(sizes.shape[0]):
        guide = guide + jnp.where(tenant == t, guidance[t], 0)
    factor = guide.astype(F32)[:, 0:1] / 4.0
    words = v_head.shape[0]
    for first in range(0, words, 512):
        last = min(first + 512, words)
        logits = dot_nt(final_input, v_head[first:last, :])
        conditional, unconditional = logits[:guided_rows], logits[guided_rows:]
        out[:, first:last] = unconditional + factor * (conditional - unconditional)


def fused(
    residual,
    queries,
    new_entries,
    key_cache,
    value_cache,
    lengths,
    attention_ids,
    expert_ids,
    attention_router,
    expert_router,
    attention_output,
    expert_gain,
    expert_gate,
    expert_up,
    expert_down,
    final_gain,
    unembedding,
    tenant_sizes,
    guidance,
):
    n_blk, n_req = lax.axis_size("blk"), lax.axis_size("req")
    n = n_blk * n_req
    requests = residual.shape[1]
    rows = queries.shape[1]
    positions = key_cache.shape[2] + 16
    width = H * HD
    vmem = pl.BlockSpec(memory_space=pltpu.VMEM)
    smem = pl.BlockSpec(memory_space=pltpu.SMEM)
    hbm = pl.BlockSpec(memory_space=pl.ANY)
    gains = jnp.stack([expert_gain, final_gain]).astype(F32)
    block = (requests, LANES)
    weights = attention_output.size + 3 * expert_gate.size + unembedding.size
    return pl.pallas_call(
        lambda *refs: step_kernel(n_blk, n_req, *refs),
        out_shape=jax.ShapeDtypeStruct((requests // 2, unembedding.shape[0]), F32),
        in_specs=[
            vmem, vmem, vmem, hbm, hbm, smem, vmem, smem, vmem, vmem, vmem,
            hbm, vmem, hbm, hbm, hbm, hbm, smem, smem,
        ],
        out_specs=vmem,
        scratch_shapes=[
            pltpu.VMEM((rows, positions, width), BF16),
            pltpu.VMEM((rows, positions, width), BF16),
            pltpu.VMEM(attention_output.shape, BF16),
            pltpu.VMEM(expert_gate.shape, BF16),
            pltpu.VMEM(expert_up.shape, BF16),
            pltpu.VMEM(expert_down.shape, BF16),
            pltpu.VMEM(unembedding.shape, BF16),
            pltpu.VMEM((n, 3 * H, LANES), BF16),
            pltpu.VMEM((n, 3 * H, LANES), BF16),
            pltpu.VMEM((requests * H // 2, LANES), F32),
            pltpu.VMEM((n, *block), BF16),
            pltpu.VMEM((n, *block), BF16),
            pltpu.VMEM(block, BF16),
            pltpu.VMEM((n, *block), BF16),
            pltpu.VMEM((n, *block), BF16),
            pltpu.VMEM((n, *block), BF16),
            pltpu.VMEM(block, BF16),
            pltpu.VMEM((2, n, *block), BF16),
            pltpu.VMEM(block, F32),
            pltpu.VMEM((expert_gate.shape[0] // 256, requests, 256), BF16),
            pltpu.SemaphoreType.DMA((2, rows)),
            pltpu.SemaphoreType.DMA((5,)),
            pltpu.SemaphoreType.DMA((4, n)),
            pltpu.SemaphoreType.DMA((4, n)),
            pltpu.SemaphoreType.DMA((2, n)),
            pltpu.SemaphoreType.DMA((2, n)),
        ],
        compiler_params=pltpu.CompilerParams(
            collective_id=0, has_side_effects=True, vmem_limit_bytes=60 * 2**20
        ),
        cost_estimate=pl.CostEstimate(
            flops=2 * requests * weights, bytes_accessed=2 * weights, transcendentals=0
        ),
    )(
        residual,
        queries,
        new_entries,
        key_cache,
        value_cache,
        lengths,
        attention_ids,
        attention_ids,
        expert_ids,
        attention_router,
        expert_router,
        attention_output,
        gains,
        expert_gate,
        expert_up,
        expert_down,
        unembedding,
        tenant_sizes,
        guidance,
    )


def solution(mesh):
    placed = (
        P("cfg", None, None),
        P("cfg", "req", None),
        P("cfg", "req", None, None),
        P("cfg", "req", "blk", None),
        P("cfg", "req", "blk", None),
        P("cfg", "req"),
        P(),
        P(),
        P(),
        P(),
        P(("blk", "req"), None),
        P(),
        P(("blk", "req"), None),
        P(("blk", "req"), None),
        P(("blk", "req"), None),
        P(),
        P(("blk", "req"), None),
        P(),
        P(),
    )
    body = fused if fits(mesh) else local
    return jax.shard_map(
        body, mesh=mesh, in_specs=placed, out_specs=P("cfg", ("blk", "req")), check_vma=False
    )
```

```python
import math

import jax
import jax.numpy as jnp
from jax import lax
from jax.experimental import pallas as pl
from jax.experimental.pallas import tpu as pltpu
from jax.sharding import PartitionSpec as P

H = 16
HD = 128
FF = 5632
TOPK = 2


EPS = 1e-05


def joined(shard, axis, combine):
    everything = jax.tree.map(
        lambda part, kind: lax.all_gather(part.astype(kind), axis),
        shard,
        (jnp.bfloat16, jnp.bfloat16, jnp.bfloat16),
    )

    def take(k):
        return jax.tree.map(lambda part, own: part[k].astype(own.dtype), everything, shard)

    return lax.fori_loop(
        1, lax.axis_size(axis), lambda k, so_far: combine(so_far, take(k)), take(0)
    )


def swapped(value, axis, bit):
    mask = 2**bit
    pairs = [(source, source ^ mask) for source in range(lax.axis_size(axis))]
    return lax.ppermute(value, axis, pairs)


def rms_scale(values):
    return values * lax.rsqrt(jnp.mean(values * values, axis=-1, keepdims=True) + EPS)


def pair_gates(logits, chosen_ids):
    experts = jnp.arange(logits.shape[-1])
    picked = jnp.sum(
        jnp.where(chosen_ids[:, :, None] == experts[None, None, :], logits[:, None, :], 0.0),
        axis=-1,
    )
    first = jax.nn.sigmoid(picked[:, 0] - picked[:, 1])
    second = jax.nn.sigmoid(picked[:, 1] - picked[:, 0])
    return jnp.stack([first, second], axis=1)


def merge_parts(first_part, second_part):
    top_first, sum_first, acc_first = first_part
    top_second, sum_second, acc_second = second_part
    highest = jnp.maximum(top_first, top_second)
    scale_first = jnp.exp(top_first - highest)
    scale_second = jnp.exp(top_second - highest)
    merged_sum = sum_first * scale_first + sum_second * scale_second
    merged_acc = acc_first * scale_first[..., None] + acc_second * scale_second[..., None]
    return (highest, merged_sum, merged_acc)


def local(
    residual,
    queries,
    new_entries,
    key_cache,
    value_cache,
    lengths,
    attention_ids,
    expert_ids,
    attention_router,
    expert_router,
    attention_output,
    expert_gain,
    expert_gate,
    expert_up,
    expert_down,
    final_gain,
    unembedding,
    tenant_sizes,
    guidance,
):
    factor_scale = 1.0 / math.sqrt(HD)
    slot_rows = queries.shape[1]
    positions_local = key_cache.shape[2]
    feature_width = H * HD
    blk_index = lax.axis_index("blk")
    linear_index = blk_index * lax.axis_size("req") + lax.axis_index("req")
    query_heads = queries[0].reshape(slot_rows, TOPK, H, HD)
    key_heads = key_cache[0].reshape(slot_rows, positions_local, H, HD)
    value_heads = value_cache[0].reshape(slot_rows, positions_local, H, HD)
    scores = (
        jnp.einsum("rkhd,rphd->rkhp", query_heads, key_heads, preferred_element_type=jnp.float32)
        * factor_scale
    )
    positions = blk_index * positions_local + jnp.arange(positions_local)
    live = (positions[None, :] < lengths[0][:, None])[:, None, None, :]
    local_top = jnp.max(jnp.where(live, scores, -1e30), axis=-1)
    weights_local = jnp.where(live, jnp.exp(scores - local_top[..., None]), 0.0)
    weight_sums = jnp.sum(weights_local, axis=-1)
    weighted = jnp.einsum(
        "rkhp,rphd->rkhd",
        weights_local.astype(jnp.bfloat16),
        value_heads,
        preferred_element_type=jnp.float32,
    )
    highest, weight_sums, weighted = joined((local_top, weight_sums, weighted), "blk", merge_parts)
    new_keys = new_entries[0][:, 0].reshape(slot_rows, H, HD)
    new_values = new_entries[0][:, 1].reshape(slot_rows, H, HD)
    new_score = (
        jnp.einsum("rkhd,rhd->rkh", query_heads, new_keys, preferred_element_type=jnp.float32)
        * factor_scale
    )
    peak = jnp.maximum(highest, new_score)
    shrink = jnp.exp(highest - peak)
    fresh = jnp.exp(new_score - peak)
    denominator = weight_sums * shrink + fresh
    fresh_rounded = fresh.astype(jnp.bfloat16)
    numerator = weighted * shrink[..., None] + jnp.einsum(
        "rkh,rhd->rkhd", fresh_rounded, new_values, preferred_element_type=jnp.float32
    )
    attention_out = (
        (numerator / denominator[..., None])
        .astype(jnp.bfloat16)
        .reshape(slot_rows, TOPK, feature_width)
    )
    inputs = residual[0].astype(jnp.float32)
    normed_input = rms_scale(inputs).astype(jnp.bfloat16)
    attention_gates = pair_gates(
        jnp.dot(normed_input, attention_router, preferred_element_type=jnp.float32), attention_ids
    )
    proj_rows = attention_output.shape[0]
    first_row = linear_index * proj_rows
    own_expert = first_row // feature_width
    own_column = first_row % feature_width
    picked = (attention_ids == own_expert).astype(jnp.float32) * attention_gates
    columns = lax.dynamic_slice_in_dim(
        lax.all_gather(attention_out, "req", axis=0, tiled=True), own_column, proj_rows, 2
    ).astype(jnp.float32)
    selected = jnp.sum(picked[:, :, None] * columns, axis=1).astype(jnp.bfloat16)
    proj_terms = jnp.dot(selected, attention_output, preferred_element_type=jnp.float32)
    attention_proj = lax.psum(proj_terms, ("blk", "req"))
    middle = inputs + attention_proj
    expert_input = (rms_scale(middle) * expert_gain.astype(jnp.float32)).astype(jnp.bfloat16)
    expert_gates = pair_gates(
        jnp.dot(expert_input, expert_router, preferred_element_type=jnp.float32), expert_ids
    )
    hidden_rows = expert_gate.shape[0]
    hidden_expert = linear_index * hidden_rows // FF
    expert_share = jnp.sum((expert_ids == hidden_expert).astype(jnp.float32) * expert_gates, axis=1)
    gate_values = jnp.einsum(
        "rd,fd->rf", expert_input, expert_gate, preferred_element_type=jnp.float32
    )
    up_values = jnp.einsum("rd,fd->rf", expert_input, expert_up, preferred_element_type=jnp.float32)
    expert_hidden = (jax.nn.silu(gate_values) * up_values * expert_share[:, None]).astype(
        jnp.bfloat16
    )
    expert_terms = jnp.dot(expert_hidden, expert_down, preferred_element_type=jnp.float32)
    expert_out = lax.psum(expert_terms, ("blk", "req"))
    final_input = (rms_scale(middle + expert_out) * final_gain.astype(jnp.float32)).astype(
        jnp.bfloat16
    )
    logits = jnp.einsum("rd,vd->rv", final_input, unembedding, preferred_element_type=jnp.float32)
    stream_index = lax.axis_index("cfg")
    half_rows = logits.shape[0] // 2
    own_rows = lax.dynamic_slice_in_dim(logits, stream_index * half_rows, half_rows, 0)
    other_rows = lax.dynamic_slice_in_dim(logits, (1 - stream_index) * half_rows, half_rows, 0)
    partner = swapped(other_rows, "cfg", 0)
    first_stream = stream_index == 0
    conditional = jnp.where(first_stream, own_rows, partner)
    unconditional = jnp.where(first_stream, partner, own_rows)
    request_index = stream_index * half_rows + jnp.arange(half_rows)
    tenant_ends = jnp.cumsum(tenant_sizes)
    tenant = jnp.sum((request_index[:, None] >= tenant_ends[None, :]).astype(jnp.int32), axis=1)
    tenant_onehot = tenant[:, None] == jnp.arange(tenant_sizes.shape[0])[None, :]
    factor = (
        jnp.sum(jnp.where(tenant_onehot, guidance[None, :], 0), axis=1).astype(jnp.float32) / 4.0
    )
    return unconditional + factor[:, None] * (conditional - unconditional)


LANES = 128
F32 = jnp.float32
BF16 = jnp.bfloat16
MESH = pl.DeviceIdType.MESH
DEAD = -1e30


def fits(mesh):
    shape = dict(mesh.shape)
    return shape["cfg"] == 2 and shape["blk"] == 4 and shape["req"] == 4


def dot_nt(left, right):
    return lax.dot_general(left, right, (((1,), (1,)), ((), ())), preferred_element_type=F32)


def expert_share_of(logits, ids, expert):
    experts = lax.broadcasted_iota(jnp.int32, logits.shape, 0)
    first = jnp.sum(jnp.where(experts == ids[0:1], logits, 0.0), axis=0, keepdims=True)
    second = jnp.sum(jnp.where(experts == ids[1:2], logits, 0.0), axis=0, keepdims=True)
    return jnp.where(ids[0:1] == expert, jax.nn.sigmoid(first - second), 0.0) + jnp.where(
        ids[1:2] == expert, jax.nn.sigmoid(second - first), 0.0
    )


def as_column(row):
    extent = row.shape[1]
    diagonal = lax.broadcasted_iota(jnp.int32, (extent, extent), 0) == lax.broadcasted_iota(
        jnp.int32, (extent, extent), 1
    )
    return jnp.sum(jnp.where(diagonal, row, 0.0), axis=1, keepdims=True)


def step_kernel(
    n_blk,
    n_req,
    residual,
    queries,
    new_entries,
    key_cache,
    value_cache,
    lengths,
    att_ids,
    att_ids_s,
    exp_ids,
    att_router,
    exp_router,
    w_proj,
    gain_in,
    gain_out,
    w_gate,
    w_up,
    w_down,
    w_head,
    sizes,
    guidance,
    out,
    keys,
    values,
    v_proj,
    v_gate,
    v_up,
    v_down,
    v_head,
    send_a,
    recv_a,
    joint,
    send_r,
    recv_r,
    send_g,
    recv_g,
    send_q,
    recv_q,
    send_f,
    recv_f,
    own_middle,
    kv_sem,
    w_sem,
    sems_s,
    sems_r,
):
    n = n_blk * n_req
    cfg = lax.axis_index("cfg")
    blk = lax.axis_index("blk")
    req = lax.axis_index("req")
    me = blk * n_req + req
    rows = queries.shape[1]
    local_pos = key_cache.shape[2]
    width = H * HD

    barrier = pltpu.get_barrier_semaphore()

    def greet(k, carry):
        other = lax.rem(me + k, n)
        for side in (0, 1):
            pl.semaphore_signal(
                barrier,
                inc=1,
                device_id=(side, other // n_req, lax.rem(other, n_req)),
                device_id_type=MESH,
            )
        return carry

    lax.fori_loop(1, n, greet, 0)
    pl.semaphore_signal(barrier, inc=1, device_id=(1 - cfg, blk, req), device_id_type=MESH)

    cache_copies = []
    for r in range(rows):
        for which, (source, target) in enumerate(((key_cache, keys), (value_cache, values))):
            copy = pltpu.make_async_copy(
                source.at[0, r], target.at[r, pl.ds(0, local_pos)], kv_sem.at[which, r]
            )
            copy.start()
            cache_copies.append(copy)
    weight_copies = []
    for source, target in (
        (w_proj, v_proj),
        (w_gate, v_gate),
        (w_up, v_up),
        (w_down, v_down),
        (w_head, v_head),
    ):
        copy = pltpu.make_async_copy(source, target, w_sem.at[len(weight_copies)])
        copy.start()
        weight_copies.append(copy)

    def start_all(source_of, target, phase):
        def go(k, carry):
            other = lax.rem(me + k, n)
            pltpu.make_async_remote_copy(
                src_ref=source_of(other),
                dst_ref=target.at[me],
                send_sem=sems_s.at[phase],
                recv_sem=sems_r.at[phase],
                device_id=(cfg, other // n_req, lax.rem(other, n_req)),
                device_id_type=MESH,
            ).start()
            return carry

        lax.fori_loop(1, n, go, 0, unroll=True)

    def all_blocks(target, phase):
        return pltpu.make_async_remote_copy(
            src_ref=target.at[pl.ds(0, n - 1)],
            dst_ref=target.at[pl.ds(0, n - 1)],
            send_sem=sems_s.at[phase],
            recv_sem=sems_r.at[phase],
            device_id=(1 - cfg, blk, req),
            device_id_type=MESH,
        )

    extra = keys.shape[1] - local_pos
    head_of_row = lax.rem(lax.broadcasted_iota(jnp.int32, (TOPK * H, 1), 0), H)
    head_of_column = lax.broadcasted_iota(jnp.int32, (TOPK * H, width), 1) // HD
    own_head = head_of_row == head_of_column
    place = lax.broadcasted_iota(jnp.int32, (1, keys.shape[1]), 1)
    new_row = lax.broadcasted_iota(jnp.int32, (extra, 1), 0) == 0
    query_all = queries[0].astype(F32)
    outs = []
    tops = []
    for copy in cache_copies:
        copy.wait()
    for r in range(rows):
        entries = new_entries[0, r].astype(F32)
        keys[r, pl.ds(local_pos, extra)] = jnp.where(new_row, entries[0:1], 0.0).astype(BF16)
        values[r, pl.ds(local_pos, extra)] = jnp.where(new_row, entries[1:2], 0.0).astype(BF16)
        spread = jnp.concatenate(
            [
                jnp.broadcast_to(query_all[r : r + 1, k * width : (k + 1) * width], (H, width))
                for k in range(TOPK)
            ],
            axis=0,
        )
        spread = jnp.where(own_head, spread, 0.0).astype(BF16)
        scores = dot_nt(spread, keys[r]) * (1.0 / math.sqrt(HD))
        cached = (place < local_pos) & (place + blk * local_pos < lengths[0, r])
        live = cached | ((place == local_pos) & (blk == 0))
        top = jnp.max(jnp.where(live, scores, DEAD), axis=1, keepdims=True)
        weights = jnp.where(live, jnp.exp(scores - top), 0.0)
        total = jnp.sum(weights, axis=1, keepdims=True)
        wide = jnp.dot(weights.astype(BF16), values[r], preferred_element_type=F32)
        acc = jnp.zeros((TOPK * H, HD), F32)
        for h in range(H):
            acc = acc + jnp.where(head_of_row == h, wide[:, h * HD : (h + 1) * HD], 0.0)
        alive = total > 0.0
        safe = jnp.where(alive, total, 1.0)
        outs.append(acc / safe)
        tops.append(jnp.where(alive, top + jnp.log(safe), DEAD))

    lane = lax.broadcasted_iota(jnp.int32, (2 * H, LANES), 1)
    half = H // 2
    for e in range(n // 2):
        picked = []
        levels = []
        for r in range(rows):
            first = jnp.where(att_ids_s[0, req * rows + r] == e, 1.0, 0.0)
            second = jnp.where(att_ids_s[1, req * rows + r] == e, 1.0, 0.0)
            picked.append(first * outs[r][:H] + second * outs[r][H:])
            levels.append(first * tops[r][:H] + second * tops[r][H:])
        for side in range(2):
            cut = slice(side * half, (side + 1) * half)
            block = jnp.concatenate([part[cut] for part in picked], axis=0)
            level = jnp.concatenate([part[cut] for part in levels], axis=0)
            high = level.astype(BF16).astype(F32)
            mid = (level - high).astype(BF16).astype(F32)
            low = level - high - mid
            parts = jnp.where(
                lax.rem(lane, 3) == 0, high, jnp.where(lax.rem(lane, 3) == 1, mid, low)
            )
            stats = jnp.where(
                lane[:H] < 3, parts[:H], jnp.where(lane[:H] < 6, parts[H:], 0.0)
            )
            send_a[2 * e + side] = jnp.concatenate([block, stats], axis=0).astype(BF16)

    pl.semaphore_wait(barrier, 2 * n - 1)
    start_all(lambda other: send_a.at[other], recv_a, 0)
    recv_a[me] = send_a[me]

    inputs = residual[0].astype(F32)
    normed = rms_scale(inputs).astype(BF16)
    att_logits = dot_nt(att_router[...], normed)
    att_share = as_column(expert_share_of(att_logits, att_ids[...], me // 2))
    weight_copies[0].wait()
    all_blocks(recv_a, 0).wait_recv()

    small = lax.broadcasted_iota(jnp.int32, (H, LANES), 1)
    for q in range(n_req):
        blocks = []
        levels = []
        for b in range(n_blk):
            message = recv_a[b * n_req + q].astype(F32)
            stats = message[2 * H :]
            upper = jnp.sum(jnp.where(small < 3, stats, 0.0), axis=1, keepdims=True)
            lower = jnp.sum(
                jnp.where((small >= 3) & (small < 6), stats, 0.0), axis=1, keepdims=True
            )
            levels.append(jnp.concatenate([upper, lower], axis=0))
            blocks.append(message[: 2 * H])
        peak = levels[0]
        for b in range(1, n_blk):
            peak = jnp.maximum(peak, levels[b])
        total = jnp.zeros_like(peak)
        mixed = jnp.zeros_like(blocks[0])
        for b in range(n_blk):
            weight = jnp.exp(levels[b] - peak)
            total = total + weight
            mixed = mixed + weight * blocks[b]
        joint[pl.ds(q * 2 * H, 2 * H)] = (mixed / total).astype(BF16).astype(F32)
    gathered = jnp.concatenate(
        [joint[pl.ds(h, n_req * rows, stride=half), :] for h in range(half)], axis=1
    )
    selected = (gathered * att_share).astype(BF16)

    def scatter(product_of, send_buf):
        for t in range(4):
            part = product_of(t)
            for j in range(4):
                send_buf[4 * t + j] = part[:, j * LANES : (j + 1) * LANES].astype(BF16)

    def summed(buf):
        total = buf[0].astype(F32)
        for k in range(1, n):
            total = total + buf[k].astype(F32)
        return total

    def whole(buf):
        return jnp.concatenate([buf[k].astype(F32) for k in range(n)], axis=1)

    def gain_row(gain):
        wide = gain[...].astype(F32)
        return jnp.concatenate([wide[k : k + 1] for k in range(n)], axis=1)

    scatter(
        lambda t: jnp.dot(
            selected, v_proj[:, t * 512 : (t + 1) * 512], preferred_element_type=F32
        ),
        send_r,
    )
    start_all(lambda other: send_r.at[other], recv_r, 1)
    recv_r[me] = send_r[me]
    all_blocks(recv_r, 1).wait_recv()
    own_column = pl.multiple_of(me * LANES, LANES)
    own_middle[...] = summed(recv_r) + residual[0, :, pl.ds(own_column, LANES)].astype(F32)
    send_g[...] = own_middle[...].astype(BF16)
    start_all(lambda other: send_g, recv_g, 2)
    recv_g[me] = send_g[...]
    weight_copies[1].wait()
    weight_copies[2].wait()
    all_blocks(recv_g, 2).wait_recv()

    expert_input = (rms_scale(whole(recv_g)) * gain_row(gain_in)).astype(BF16)
    share = expert_share_of(
        dot_nt(exp_router[...], expert_input), exp_ids[...], me * v_gate.shape[0] // FF
    )
    tile = v_gate.shape[0] // 2
    pieces = []
    for t in range(2):
        gate_values = dot_nt(v_gate[t * tile : (t + 1) * tile, :], expert_input)
        up_values = dot_nt(v_up[t * tile : (t + 1) * tile, :], expert_input)
        part = jax.nn.silu(gate_values) * up_values * share
        pieces.append(jnp.transpose(part).astype(BF16))
    weight_copies[3].wait()
    all_hidden = jnp.concatenate(pieces, axis=1)
    scatter(
        lambda t: jnp.dot(
            all_hidden, v_down[:, t * 512 : (t + 1) * 512], preferred_element_type=F32
        ),
        send_q,
    )
    start_all(lambda other: send_q.at[other], recv_q, 3)
    recv_q[me] = send_q[me]
    all_blocks(recv_q, 3).wait_recv()
    send_f[...] = (own_middle[...] + summed(recv_q)).astype(BF16)

    def final_send(away, other):
        side = 1 - cfg if away else cfg
        pltpu.make_async_remote_copy(
            src_ref=send_f,
            dst_ref=recv_f.at[cfg, me],
            send_sem=sems_s.at[4 + away],
            recv_sem=sems_r.at[4 + away],
            device_id=(side, other // n_req, lax.rem(other, n_req)),
            device_id_type=MESH,
        ).start()

    def final_step(k, carry):
        other = lax.rem(me + k, n)
        final_send(0, other)
        final_send(1, other)
        return carry

    lax.fori_loop(1, n, final_step, 0, unroll=True)
    final_send(1, me)
    recv_f[cfg, me] = send_f[...]
    weight_copies[4].wait()
    for away in (0, 1):
        target = recv_f.at[0, pl.ds(0, n - 1 + away)]
        pltpu.make_async_remote_copy(
            src_ref=target,
            dst_ref=target,
            send_sem=sems_s.at[4 + away],
            recv_sem=sems_r.at[4 + away],
            device_id=(1 - cfg, blk, req),
            device_id_type=MESH,
        ).wait()
    for phase, target in enumerate((recv_a, recv_r, recv_g, recv_q)):
        all_blocks(target, phase).wait_send()

    guided_rows = out.shape[0]
    mine = []
    for stream in (0, 1):
        both = whole(recv_f.at[stream])
        mine.append(jnp.where(cfg == 0, both[:guided_rows], both[guided_rows:]))
    final_input = (rms_scale(jnp.concatenate(mine, axis=0)) * gain_row(gain_out)).astype(BF16)
    request = cfg * guided_rows + lax.broadcasted_iota(jnp.int32, (guided_rows, LANES), 0)
    tenant = jnp.zeros_like(request)
    end = 0
    for t in range(sizes.shape[0]):
        end = end + sizes[t]
        tenant = tenant + jnp.where(request >= end, 1, 0)
    guide = jnp.zeros_like(request)
    for t in range(sizes.shape[0]):
        guide = guide + jnp.where(tenant == t, guidance[t], 0)
    factor = guide.astype(F32)[:, 0:1] / 4.0
    words = v_head.shape[0]
    for first in range(0, words, 1024):
        last = min(first + 1024, words)
        logits = jnp.transpose(dot_nt(v_head[first:last, :], final_input))
        conditional, unconditional = logits[:guided_rows], logits[guided_rows:]
        out[:, first:last] = unconditional + factor * (conditional - unconditional)


def fused(
    residual,
    queries,
    new_entries,
    key_cache,
    value_cache,
    lengths,
    attention_ids,
    expert_ids,
    attention_router,
    expert_router,
    attention_output,
    expert_gain,
    expert_gate,
    expert_up,
    expert_down,
    final_gain,
    unembedding,
    tenant_sizes,
    guidance,
):
    n_blk, n_req = lax.axis_size("blk"), lax.axis_size("req")
    n = n_blk * n_req
    requests = residual.shape[1]
    rows = queries.shape[1]
    positions = key_cache.shape[2] + 16
    width = H * HD
    vmem = pl.BlockSpec(memory_space=pltpu.VMEM)
    smem = pl.BlockSpec(memory_space=pltpu.SMEM)
    hbm = pl.BlockSpec(memory_space=pl.ANY)
    block = (requests, LANES)
    weights = attention_output.size + 3 * expert_gate.size + unembedding.size
    return pl.pallas_call(
        lambda *refs: step_kernel(n_blk, n_req, *refs),
        out_shape=jax.ShapeDtypeStruct((requests // 2, unembedding.shape[0]), F32),
        in_specs=[
            vmem, vmem, vmem, hbm, hbm, smem, vmem, smem, vmem, vmem, vmem,
            hbm, vmem, vmem, hbm, hbm, hbm, hbm, smem, smem,
        ],
        out_specs=vmem,
        scratch_shapes=[
            pltpu.VMEM((rows, positions, width), BF16),
            pltpu.VMEM((rows, positions, width), BF16),
            pltpu.VMEM(attention_output.shape, BF16),
            pltpu.VMEM(expert_gate.shape, BF16),
            pltpu.VMEM(expert_up.shape, BF16),
            pltpu.VMEM(expert_down.shape, BF16),
            pltpu.VMEM(unembedding.shape, BF16),
            pltpu.VMEM((n, 3 * H, LANES), BF16),
            pltpu.VMEM((n, 3 * H, LANES), BF16),
            pltpu.VMEM((requests * H // 2, LANES), F32),
            pltpu.VMEM((n, *block), BF16),
            pltpu.VMEM((n, *block), BF16),
            pltpu.VMEM(block, BF16),
            pltpu.VMEM((n, *block), BF16),
            pltpu.VMEM((n, *block), BF16),
            pltpu.VMEM((n, *block), BF16),
            pltpu.VMEM(block, BF16),
            pltpu.VMEM((2, n, *block), BF16),
            pltpu.VMEM(block, F32),
            pltpu.SemaphoreType.DMA((2, rows)),
            pltpu.SemaphoreType.DMA((5,)),
            pltpu.SemaphoreType.DMA((6,)),
            pltpu.SemaphoreType.DMA((6,)),
        ],
        compiler_params=pltpu.CompilerParams(
            collective_id=0, has_side_effects=True, vmem_limit_bytes=60 * 2**20
        ),
        cost_estimate=pl.CostEstimate(
            flops=2 * requests * weights, bytes_accessed=2 * weights, transcendentals=0
        ),
    )(
        residual,
        queries,
        new_entries,
        key_cache,
        value_cache,
        lengths,
        attention_ids.T,
        attention_ids.T,
        expert_ids.T,
        attention_router.T,
        expert_router.T,
        attention_output,
        expert_gain.reshape(n, LANES),
        final_gain.reshape(n, LANES),
        expert_gate,
        expert_up,
        expert_down,
        unembedding,
        tenant_sizes,
        guidance,
    )


def solution(mesh):
    placed = (
        P("cfg", None, None),
        P("cfg", "req", None),
        P("cfg", "req", None, None),
        P("cfg", "req", "blk", None),
        P("cfg", "req", "blk", None),
        P("cfg", "req"),
        P(),
        P(),
        P(),
        P(),
        P(("blk", "req"), None),
        P(),
        P(("blk", "req"), None),
        P(("blk", "req"), None),
        P(("blk", "req"), None),
        P(),
        P(("blk", "req"), None),
        P(),
        P(),
    )
    body = fused if fits(mesh) else local
    return jax.shard_map(
        body, mesh=mesh, in_specs=placed, out_specs=P("cfg", ("blk", "req")), check_vma=False
    )
```

```python
import math

import jax
import jax.numpy as jnp
from jax import lax
from jax.experimental import pallas as pl
from jax.experimental.pallas import tpu as pltpu
from jax.sharding import PartitionSpec as P

H = 16
HD = 128
FF = 5632
TOPK = 2


EPS = 1e-05


def joined(shard, axis, combine):
    everything = jax.tree.map(
        lambda part, kind: lax.all_gather(part.astype(kind), axis),
        shard,
        (jnp.bfloat16, jnp.bfloat16, jnp.bfloat16),
    )

    def take(k):
        return jax.tree.map(lambda part, own: part[k].astype(own.dtype), everything, shard)

    return lax.fori_loop(
        1, lax.axis_size(axis), lambda k, so_far: combine(so_far, take(k)), take(0)
    )


def swapped(value, axis, bit):
    mask = 2**bit
    pairs = [(source, source ^ mask) for source in range(lax.axis_size(axis))]
    return lax.ppermute(value, axis, pairs)


def rms_scale(values):
    return values * lax.rsqrt(jnp.mean(values * values, axis=-1, keepdims=True) + EPS)


def pair_gates(logits, chosen_ids):
    experts = jnp.arange(logits.shape[-1])
    picked = jnp.sum(
        jnp.where(chosen_ids[:, :, None] == experts[None, None, :], logits[:, None, :], 0.0),
        axis=-1,
    )
    first = jax.nn.sigmoid(picked[:, 0] - picked[:, 1])
    second = jax.nn.sigmoid(picked[:, 1] - picked[:, 0])
    return jnp.stack([first, second], axis=1)


def merge_parts(first_part, second_part):
    top_first, sum_first, acc_first = first_part
    top_second, sum_second, acc_second = second_part
    highest = jnp.maximum(top_first, top_second)
    scale_first = jnp.exp(top_first - highest)
    scale_second = jnp.exp(top_second - highest)
    merged_sum = sum_first * scale_first + sum_second * scale_second
    merged_acc = acc_first * scale_first[..., None] + acc_second * scale_second[..., None]
    return (highest, merged_sum, merged_acc)


def local(
    residual,
    queries,
    new_entries,
    key_cache,
    value_cache,
    lengths,
    attention_ids,
    expert_ids,
    attention_router,
    expert_router,
    attention_output,
    expert_gain,
    expert_gate,
    expert_up,
    expert_down,
    final_gain,
    unembedding,
    tenant_sizes,
    guidance,
):
    factor_scale = 1.0 / math.sqrt(HD)
    slot_rows = queries.shape[1]
    positions_local = key_cache.shape[2]
    feature_width = H * HD
    blk_index = lax.axis_index("blk")
    linear_index = blk_index * lax.axis_size("req") + lax.axis_index("req")
    query_heads = queries[0].reshape(slot_rows, TOPK, H, HD)
    key_heads = key_cache[0].reshape(slot_rows, positions_local, H, HD)
    value_heads = value_cache[0].reshape(slot_rows, positions_local, H, HD)
    scores = (
        jnp.einsum("rkhd,rphd->rkhp", query_heads, key_heads, preferred_element_type=jnp.float32)
        * factor_scale
    )
    positions = blk_index * positions_local + jnp.arange(positions_local)
    live = (positions[None, :] < lengths[0][:, None])[:, None, None, :]
    local_top = jnp.max(jnp.where(live, scores, -1e30), axis=-1)
    weights_local = jnp.where(live, jnp.exp(scores - local_top[..., None]), 0.0)
    weight_sums = jnp.sum(weights_local, axis=-1)
    weighted = jnp.einsum(
        "rkhp,rphd->rkhd",
        weights_local.astype(jnp.bfloat16),
        value_heads,
        preferred_element_type=jnp.float32,
    )
    highest, weight_sums, weighted = joined((local_top, weight_sums, weighted), "blk", merge_parts)
    new_keys = new_entries[0][:, 0].reshape(slot_rows, H, HD)
    new_values = new_entries[0][:, 1].reshape(slot_rows, H, HD)
    new_score = (
        jnp.einsum("rkhd,rhd->rkh", query_heads, new_keys, preferred_element_type=jnp.float32)
        * factor_scale
    )
    peak = jnp.maximum(highest, new_score)
    shrink = jnp.exp(highest - peak)
    fresh = jnp.exp(new_score - peak)
    denominator = weight_sums * shrink + fresh
    fresh_rounded = fresh.astype(jnp.bfloat16)
    numerator = weighted * shrink[..., None] + jnp.einsum(
        "rkh,rhd->rkhd", fresh_rounded, new_values, preferred_element_type=jnp.float32
    )
    attention_out = (
        (numerator / denominator[..., None])
        .astype(jnp.bfloat16)
        .reshape(slot_rows, TOPK, feature_width)
    )
    inputs = residual[0].astype(jnp.float32)
    normed_input = rms_scale(inputs).astype(jnp.bfloat16)
    attention_gates = pair_gates(
        jnp.dot(normed_input, attention_router, preferred_element_type=jnp.float32), attention_ids
    )
    proj_rows = attention_output.shape[0]
    first_row = linear_index * proj_rows
    own_expert = first_row // feature_width
    own_column = first_row % feature_width
    picked = (attention_ids == own_expert).astype(jnp.float32) * attention_gates
    columns = lax.dynamic_slice_in_dim(
        lax.all_gather(attention_out, "req", axis=0, tiled=True), own_column, proj_rows, 2
    ).astype(jnp.float32)
    selected = jnp.sum(picked[:, :, None] * columns, axis=1).astype(jnp.bfloat16)
    proj_terms = jnp.dot(selected, attention_output, preferred_element_type=jnp.float32)
    attention_proj = lax.psum(proj_terms, ("blk", "req"))
    middle = inputs + attention_proj
    expert_input = (rms_scale(middle) * expert_gain.astype(jnp.float32)).astype(jnp.bfloat16)
    expert_gates = pair_gates(
        jnp.dot(expert_input, expert_router, preferred_element_type=jnp.float32), expert_ids
    )
    hidden_rows = expert_gate.shape[0]
    hidden_expert = linear_index * hidden_rows // FF
    expert_share = jnp.sum((expert_ids == hidden_expert).astype(jnp.float32) * expert_gates, axis=1)
    gate_values = jnp.einsum(
        "rd,fd->rf", expert_input, expert_gate, preferred_element_type=jnp.float32
    )
    up_values = jnp.einsum("rd,fd->rf", expert_input, expert_up, preferred_element_type=jnp.float32)
    expert_hidden = (jax.nn.silu(gate_values) * up_values * expert_share[:, None]).astype(
        jnp.bfloat16
    )
    expert_terms = jnp.dot(expert_hidden, expert_down, preferred_element_type=jnp.float32)
    expert_out = lax.psum(expert_terms, ("blk", "req"))
    final_input = (rms_scale(middle + expert_out) * final_gain.astype(jnp.float32)).astype(
        jnp.bfloat16
    )
    logits = jnp.einsum("rd,vd->rv", final_input, unembedding, preferred_element_type=jnp.float32)
    stream_index = lax.axis_index("cfg")
    half_rows = logits.shape[0] // 2
    own_rows = lax.dynamic_slice_in_dim(logits, stream_index * half_rows, half_rows, 0)
    other_rows = lax.dynamic_slice_in_dim(logits, (1 - stream_index) * half_rows, half_rows, 0)
    partner = swapped(other_rows, "cfg", 0)
    first_stream = stream_index == 0
    conditional = jnp.where(first_stream, own_rows, partner)
    unconditional = jnp.where(first_stream, partner, own_rows)
    request_index = stream_index * half_rows + jnp.arange(half_rows)
    tenant_ends = jnp.cumsum(tenant_sizes)
    tenant = jnp.sum((request_index[:, None] >= tenant_ends[None, :]).astype(jnp.int32), axis=1)
    tenant_onehot = tenant[:, None] == jnp.arange(tenant_sizes.shape[0])[None, :]
    factor = (
        jnp.sum(jnp.where(tenant_onehot, guidance[None, :], 0), axis=1).astype(jnp.float32) / 4.0
    )
    return unconditional + factor[:, None] * (conditional - unconditional)


LANES = 128
F32 = jnp.float32
BF16 = jnp.bfloat16
MESH = pl.DeviceIdType.MESH
DEAD = -1e30


def fits(mesh):
    shape = dict(mesh.shape)
    return shape["cfg"] == 2 and shape["blk"] == 4 and shape["req"] == 4


def dot_nt(left, right):
    return lax.dot_general(left, right, (((1,), (1,)), ((), ())), preferred_element_type=F32)


def expert_share_of(logits, ids, expert):
    experts = lax.broadcasted_iota(jnp.int32, logits.shape, 0)
    first = jnp.sum(jnp.where(experts == ids[0:1], logits, 0.0), axis=0, keepdims=True)
    second = jnp.sum(jnp.where(experts == ids[1:2], logits, 0.0), axis=0, keepdims=True)
    return jnp.where(ids[0:1] == expert, jax.nn.sigmoid(first - second), 0.0) + jnp.where(
        ids[1:2] == expert, jax.nn.sigmoid(second - first), 0.0
    )


def as_column(row):
    extent = row.shape[1]
    diagonal = lax.broadcasted_iota(jnp.int32, (extent, extent), 0) == lax.broadcasted_iota(
        jnp.int32, (extent, extent), 1
    )
    return jnp.sum(jnp.where(diagonal, row, 0.0), axis=1, keepdims=True)


def as_row(column):
    extent = column.shape[0]
    diagonal = lax.broadcasted_iota(jnp.int32, (extent, extent), 0) == lax.broadcasted_iota(
        jnp.int32, (extent, extent), 1
    )
    return jnp.sum(jnp.where(diagonal, column, 0.0), axis=0, keepdims=True)


def step_kernel(
    n_blk,
    n_req,
    residual,
    queries,
    new_entries,
    key_cache,
    value_cache,
    lengths,
    att_ids,
    att_ids_s,
    exp_ids,
    att_router,
    exp_router,
    w_proj,
    gain_in,
    gain_out,
    w_gate,
    w_up,
    w_down,
    w_head,
    sizes,
    guidance,
    out,
    keys,
    values,
    v_proj,
    v_gate,
    v_up,
    v_down,
    v_head,
    send_a,
    recv_a,
    joint,
    send_r,
    recv_r,
    send_g,
    recv_g,
    send_q,
    recv_q,
    send_f,
    recv_f,
    own_middle,
    kv_sem,
    w_sem,
    sems_s,
    sems_r,
    sems_g,
    sems_f,
    gain_rows,
):
    n = n_blk * n_req
    cfg = lax.axis_index("cfg")
    blk = lax.axis_index("blk")
    req = lax.axis_index("req")
    me = blk * n_req + req
    rows = queries.shape[1]
    local_pos = key_cache.shape[2]
    width = H * HD

    barrier = pltpu.get_barrier_semaphore()

    def greet(k, carry):
        other = lax.rem(me + k, n)
        for side in (0, 1):
            pl.semaphore_signal(
                barrier,
                inc=1,
                device_id=(side, other // n_req, lax.rem(other, n_req)),
                device_id_type=MESH,
            )
        return carry

    lax.fori_loop(1, n, greet, 0)
    pl.semaphore_signal(barrier, inc=1, device_id=(1 - cfg, blk, req), device_id_type=MESH)

    cache_copies = []
    for r in range(rows):
        for which, (source, target) in enumerate(((key_cache, keys), (value_cache, values))):
            copy = pltpu.make_async_copy(
                source.at[0, r], target.at[r, pl.ds(0, local_pos)], kv_sem.at[which, r]
            )
            copy.start()
            cache_copies.append(copy)
    weight_copies = []
    for source, target in (
        (w_proj, v_proj),
        (w_gate, v_gate),
        (w_up, v_up),
        (w_down, v_down),
        (w_head, v_head),
    ):
        extent = source.shape[0]
        sem = w_sem.at[len(weight_copies)]
        for first in range(0, extent, 512):
            cut = pl.ds(first, min(512, extent - first))
            pltpu.make_async_copy(source.at[cut], target.at[cut], sem).start()
        weight_copies.append(pltpu.make_async_copy(source, target, sem))

    upper = blk // 2
    near = (blk, 4 * upper + 1 - blk, 2 - upper, 3 - 3 * upper)
    columns = n_req * LANES

    def send_plane(source_of, target, plane, own, side, send_sem, recv_sem):
        def go(k, carry):
            to = lax.rem(req + k, n_req)
            pltpu.make_async_remote_copy(
                src_ref=source_of(plane * n_req + to),
                dst_ref=target.at[me],
                send_sem=send_sem,
                recv_sem=recv_sem,
                device_id=(side, plane, to),
                device_id_type=MESH,
            ).start()
            return carry

        lax.fori_loop(1 if own else 0, n_req, go, 0, unroll=True)

    def wait_plane(target, count, sem):
        blocks = target.at[pl.ds(0, count)]
        pltpu.make_async_remote_copy(
            src_ref=blocks,
            dst_ref=blocks,
            send_sem=sem,
            recv_sem=sem,
            device_id=(1 - cfg, blk, req),
            device_id_type=MESH,
        ).wait_recv()

    def plane_of(buf, plane):
        return jnp.concatenate(
            [buf[plane * n_req + j].astype(F32) for j in range(n_req)], axis=1
        )

    def gain_of(buf, plane):
        return jnp.concatenate(
            [buf[pl.ds(plane * n_req + j, 1), :] for j in range(n_req)], axis=1
        )

    def columns_of(plane):
        return pl.ds(pl.multiple_of(plane * columns, columns), columns)

    def start_all(source_of, target, phase):
        def go(k, carry):
            other = lax.rem(me + k, n)
            pltpu.make_async_remote_copy(
                src_ref=source_of(other),
                dst_ref=target.at[me],
                send_sem=sems_s.at[phase],
                recv_sem=sems_r.at[phase],
                device_id=(cfg, other // n_req, lax.rem(other, n_req)),
                device_id_type=MESH,
            ).start()
            return carry

        lax.fori_loop(1, n, go, 0, unroll=True)

    def all_blocks(target, phase):
        return pltpu.make_async_remote_copy(
            src_ref=target.at[pl.ds(0, n - 1)],
            dst_ref=target.at[pl.ds(0, n - 1)],
            send_sem=sems_s.at[phase],
            recv_sem=sems_r.at[phase],
            device_id=(1 - cfg, blk, req),
            device_id_type=MESH,
        )

    extra = keys.shape[1] - local_pos
    head_of_row = lax.rem(lax.broadcasted_iota(jnp.int32, (TOPK * H, 1), 0), H)
    head_of_column = lax.broadcasted_iota(jnp.int32, (TOPK * H, width), 1) // HD
    own_head = head_of_row == head_of_column
    place = lax.broadcasted_iota(jnp.int32, (1, keys.shape[1]), 1)
    new_row = lax.broadcasted_iota(jnp.int32, (extra, 1), 0) == 0
    query_all = queries[0].astype(F32)
    outs = []
    tops = []
    for copy in cache_copies:
        copy.wait()
    for r in range(rows):
        entries = new_entries[0, r].astype(F32)
        keys[r, pl.ds(local_pos, extra)] = jnp.where(new_row, entries[0:1], 0.0).astype(BF16)
        values[r, pl.ds(local_pos, extra)] = jnp.where(new_row, entries[1:2], 0.0).astype(BF16)
        spread = jnp.concatenate(
            [
                jnp.broadcast_to(query_all[r : r + 1, k * width : (k + 1) * width], (H, width))
                for k in range(TOPK)
            ],
            axis=0,
        )
        spread = jnp.where(own_head, spread, 0.0).astype(BF16)
        scores = dot_nt(spread, keys[r]) * (1.0 / math.sqrt(HD))
        cached = (place < local_pos) & (place + blk * local_pos < lengths[0, r])
        live = cached | ((place == local_pos) & (blk == 0))
        top = jnp.max(jnp.where(live, scores, DEAD), axis=1, keepdims=True)
        weights = jnp.where(live, jnp.exp(scores - top), 0.0)
        total = jnp.sum(weights, axis=1, keepdims=True)
        wide = jnp.dot(weights.astype(BF16), values[r], preferred_element_type=F32)
        acc = jnp.zeros((TOPK * H, HD), F32)
        for h in range(H):
            acc = acc + jnp.where(head_of_row == h, wide[:, h * HD : (h + 1) * HD], 0.0)
        alive = total > 0.0
        safe = jnp.where(alive, total, 1.0)
        outs.append(acc / safe)
        tops.append(jnp.where(alive, top + jnp.log(safe), DEAD))

    lane = lax.broadcasted_iota(jnp.int32, (2 * H, LANES), 1)
    half = H // 2
    for e in range(n // 2):
        picked = []
        levels = []
        for r in range(rows):
            first = jnp.where(att_ids_s[0, req * rows + r] == e, 1.0, 0.0)
            second = jnp.where(att_ids_s[1, req * rows + r] == e, 1.0, 0.0)
            picked.append(first * outs[r][:H] + second * outs[r][H:])
            levels.append(first * tops[r][:H] + second * tops[r][H:])
        for side in range(2):
            cut = slice(side * half, (side + 1) * half)
            block = jnp.concatenate([part[cut] for part in picked], axis=0)
            level = jnp.concatenate([part[cut] for part in levels], axis=0)
            high = level.astype(BF16).astype(F32)
            mid = (level - high).astype(BF16).astype(F32)
            low = level - high - mid
            parts = jnp.where(
                lax.rem(lane, 3) == 0, high, jnp.where(lax.rem(lane, 3) == 1, mid, low)
            )
            stats = jnp.where(
                lane[:H] < 3, parts[:H], jnp.where(lane[:H] < 6, parts[H:], 0.0)
            )
            send_a[2 * e + side] = jnp.concatenate([block, stats], axis=0).astype(BF16)

    pl.semaphore_wait(barrier, 2 * n - 1)

    @pl.when(cfg * blk == 0)
    def _():
        start_all(lambda other: send_a.at[other], recv_a, 0)

    @pl.when(cfg == 1)
    def _():
        spot = (n - n_req, 3 * H, LANES)
        row = lax.broadcasted_iota(jnp.int32, spot, 1)
        column = lax.broadcasted_iota(jnp.int32, spot, 2)
        empty = (row >= 2 * H) & ((column == 0) | (column == 3))
        recv_a[pl.ds(n_req, n - n_req)] = jnp.where(empty, DEAD, 0.0).astype(BF16)

    recv_a[me] = send_a[me]
    gain_rows[0] = gain_in[...].astype(F32)
    gain_rows[1] = gain_out[...].astype(F32)

    inputs = residual[0].astype(F32)
    normed = rms_scale(inputs).astype(BF16)
    att_logits = dot_nt(att_router[...], normed)
    att_share = as_column(expert_share_of(att_logits, att_ids[...], me // 2))
    weight_copies[0].wait()

    @pl.when(cfg == 0)
    def _():
        wait_plane(recv_a, n - 1, sems_r.at[0])

    @pl.when(cfg * (blk + 1) == 1)
    def _():
        wait_plane(recv_a, n_req - 1, sems_r.at[0])

    @pl.when(cfg * blk > 0)
    def _():
        wait_plane(recv_a, n_req, sems_r.at[0])


    small = lax.broadcasted_iota(jnp.int32, (H, LANES), 1)
    for q in range(n_req):
        blocks = []
        levels = []
        for b in range(n_blk):
            message = recv_a[b * n_req + q].astype(F32)
            stats = message[2 * H :]
            upper = jnp.sum(jnp.where(small < 3, stats, 0.0), axis=1, keepdims=True)
            lower = jnp.sum(
                jnp.where((small >= 3) & (small < 6), stats, 0.0), axis=1, keepdims=True
            )
            levels.append(jnp.concatenate([upper, lower], axis=0))
            blocks.append(message[: 2 * H])
        peak = levels[0]
        for b in range(1, n_blk):
            peak = jnp.maximum(peak, levels[b])
        total = jnp.zeros_like(peak)
        mixed = jnp.zeros_like(blocks[0])
        for b in range(n_blk):
            weight = jnp.exp(levels[b] - peak)
            total = total + weight
            mixed = mixed + weight * blocks[b]
        joint[pl.ds(q * 2 * H, 2 * H)] = (mixed / total).astype(BF16).astype(F32)
    gathered = jnp.concatenate(
        [joint[pl.ds(h, n_req * rows, stride=half), :] for h in range(half)], axis=1
    )
    selected = (gathered * att_share).astype(BF16)

    def scatter(left, weights, send_buf, target, phase):
        for step in range(n_blk):
            plane = near[n_blk - 1 - step]
            part = jnp.dot(left, weights[:, columns_of(plane)], preferred_element_type=F32)
            for j in range(n_req):
                send_buf[plane * n_req + j] = part[:, j * LANES : (j + 1) * LANES].astype(BF16)
            send_plane(
                lambda other: send_buf.at[other],
                target,
                plane,
                step == n_blk - 1,
                cfg,
                sems_s.at[phase],
                sems_r.at[phase],
            )
        target[me] = send_buf[me]
        all_blocks(target, phase).wait_recv()

    def summed(buf):
        total = buf[0].astype(F32)
        for k in range(1, n):
            total = total + buf[k].astype(F32)
        return total

    def squares(values):
        return jnp.sum(values * values, axis=1, keepdims=True)

    scatter(selected, v_proj, send_r, recv_r, 1)
    own_column = pl.multiple_of(me * LANES, LANES)
    own_middle[...] = summed(recv_r) + residual[0, :, pl.ds(own_column, LANES)].astype(F32)
    send_g[...] = own_middle[...].astype(BF16)
    for step in range(n_blk):
        plane = near[n_blk - 1 - step]
        send_plane(
            lambda other: send_g, recv_g, plane, step == n_blk - 1, cfg, sems_s.at[2], sems_g.at[blk]
        )
    recv_g[me] = send_g[...]
    weight_copies[1].wait()
    weight_copies[2].wait()
    square_sum = 0.0
    gate_sum = 0.0
    up_sum = 0.0
    router_sum = 0.0
    for step in range(n_blk):
        plane = near[step]
        wait_plane(recv_g, n_req - 1 if step == 0 else n_req, sems_g.at[plane])
        part = plane_of(recv_g, plane)
        square_sum = square_sum + squares(part)
        part = (part * gain_of(gain_rows.at[0], plane)).astype(BF16)
        gate_sum = gate_sum + dot_nt(part, v_gate[:, columns_of(plane)])
        up_sum = up_sum + dot_nt(part, v_up[:, columns_of(plane)])
        router_sum = router_sum + dot_nt(exp_router[:, columns_of(plane)], part)
    scale = lax.rsqrt(square_sum / (n * LANES) + EPS)
    share = as_column(
        expert_share_of(
            router_sum * as_row(scale), exp_ids[...], me * v_gate.shape[0] // FF
        )
    )
    all_hidden = (jax.nn.silu(gate_sum * scale) * (up_sum * (scale * share))).astype(BF16)
    weight_copies[3].wait()
    scatter(all_hidden, v_down, send_q, recv_q, 3)
    send_f[...] = (own_middle[...] + summed(recv_q)).astype(BF16)
    for step in range(n_blk):
        plane = near[n_blk - 1 - step]
        for away in (0, 1):
            send_plane(
                lambda other: send_f,
                recv_f.at[cfg],
                plane,
                step == n_blk - 1 and away == 0,
                1 - cfg if away else cfg,
                sems_s.at[4 + away],
                sems_f.at[away, blk],
            )
    recv_f[cfg, me] = send_f[...]
    weight_copies[4].wait()

    guided_rows = out.shape[0]
    request = cfg * guided_rows + lax.broadcasted_iota(jnp.int32, (guided_rows, LANES), 0)
    tenant = jnp.zeros_like(request)
    end = 0
    for t in range(sizes.shape[0]):
        end = end + sizes[t]
        tenant = tenant + jnp.where(request >= end, 1, 0)
    guide = jnp.zeros_like(request)
    for t in range(sizes.shape[0]):
        guide = guide + jnp.where(tenant == t, guidance[t], 0)
    factor = guide.astype(F32)[:, 0:1] / 4.0
    square_sum = 0.0
    logits = 0.0
    for step in range(n_blk):
        plane = near[step]
        for away in (0, 1):
            wait_plane(
                recv_f.at[0],
                n_req - 1 if step == 0 and away == 0 else n_req,
                sems_f.at[away, plane],
            )
        mine = []
        for stream in (0, 1):
            both = plane_of(recv_f.at[stream], plane)
            mine.append(jnp.where(cfg == 0, both[:guided_rows], both[guided_rows:]))
        part = jnp.concatenate(mine, axis=0)
        square_sum = square_sum + squares(part)
        part = (part * gain_of(gain_rows.at[1], plane)).astype(BF16)
        logits = logits + dot_nt(part, v_head[:, columns_of(plane)])
    logits = logits * lax.rsqrt(square_sum / (n * LANES) + EPS)
    conditional, unconditional = logits[:guided_rows], logits[guided_rows:]
    out[...] = unconditional + factor * (conditional - unconditional)

    @pl.when(cfg * blk == 0)
    def _():
        all_blocks(recv_a, 0).wait_send()

    for phase, target in ((1, recv_r), (2, recv_g), (3, recv_q), (4, recv_f.at[0])):
        all_blocks(target, phase).wait_send()
    pltpu.make_async_remote_copy(
        src_ref=recv_f.at[0],
        dst_ref=recv_f.at[0],
        send_sem=sems_s.at[5],
        recv_sem=sems_r.at[0],
        device_id=(1 - cfg, blk, req),
        device_id_type=MESH,
    ).wait_send()


def fused(
    residual,
    queries,
    new_entries,
    key_cache,
    value_cache,
    lengths,
    attention_ids,
    expert_ids,
    attention_router,
    expert_router,
    attention_output,
    expert_gain,
    expert_gate,
    expert_up,
    expert_down,
    final_gain,
    unembedding,
    tenant_sizes,
    guidance,
):
    n_blk, n_req = lax.axis_size("blk"), lax.axis_size("req")
    n = n_blk * n_req
    requests = residual.shape[1]
    rows = queries.shape[1]
    positions = key_cache.shape[2] + 16
    width = H * HD
    vmem = pl.BlockSpec(memory_space=pltpu.VMEM)
    smem = pl.BlockSpec(memory_space=pltpu.SMEM)
    hbm = pl.BlockSpec(memory_space=pl.ANY)
    block = (requests, LANES)
    weights = attention_output.size + 3 * expert_gate.size + unembedding.size
    return pl.pallas_call(
        lambda *refs: step_kernel(n_blk, n_req, *refs),
        out_shape=jax.ShapeDtypeStruct((requests // 2, unembedding.shape[0]), F32),
        in_specs=[
            vmem, vmem, vmem, hbm, hbm, smem, vmem, smem, vmem, vmem, vmem,
            hbm, vmem, vmem, hbm, hbm, hbm, hbm, smem, smem,
        ],
        out_specs=vmem,
        scratch_shapes=[
            pltpu.VMEM((rows, positions, width), BF16),
            pltpu.VMEM((rows, positions, width), BF16),
            pltpu.VMEM(attention_output.shape, BF16),
            pltpu.VMEM(expert_gate.shape, BF16),
            pltpu.VMEM(expert_up.shape, BF16),
            pltpu.VMEM(expert_down.shape, BF16),
            pltpu.VMEM(unembedding.shape, BF16),
            pltpu.VMEM((n, 3 * H, LANES), BF16),
            pltpu.VMEM((n, 3 * H, LANES), BF16),
            pltpu.VMEM((requests * H // 2, LANES), F32),
            pltpu.VMEM((n, *block), BF16),
            pltpu.VMEM((n, *block), BF16),
            pltpu.VMEM(block, BF16),
            pltpu.VMEM((n, *block), BF16),
            pltpu.VMEM((n, *block), BF16),
            pltpu.VMEM((n, *block), BF16),
            pltpu.VMEM(block, BF16),
            pltpu.VMEM((2, n, *block), BF16),
            pltpu.VMEM(block, F32),
            pltpu.SemaphoreType.DMA((2, rows)),
            pltpu.SemaphoreType.DMA((5,)),
            pltpu.SemaphoreType.DMA((6,)),
            pltpu.SemaphoreType.DMA((4,)),
            pltpu.SemaphoreType.DMA((n_blk,)),
            pltpu.SemaphoreType.DMA((2, n_blk)),
            pltpu.VMEM((2, n, LANES), F32),
        ],
        compiler_params=pltpu.CompilerParams(
            collective_id=0, has_side_effects=True, vmem_limit_bytes=60 * 2**20
        ),
        cost_estimate=pl.CostEstimate(
            flops=2 * requests * weights, bytes_accessed=2 * weights, transcendentals=0
        ),
    )(
        residual,
        queries,
        new_entries,
        key_cache,
        value_cache,
        lengths,
        attention_ids.T,
        attention_ids.T,
        expert_ids.T,
        attention_router.T,
        expert_router.T,
        attention_output,
        expert_gain.reshape(n, LANES),
        final_gain.reshape(n, LANES),
        expert_gate,
        expert_up,
        expert_down,
        unembedding,
        tenant_sizes,
        guidance,
    )


def solution(mesh):
    placed = (
        P("cfg", None, None),
        P("cfg", "req", None),
        P("cfg", "req", None, None),
        P("cfg", "req", "blk", None),
        P("cfg", "req", "blk", None),
        P("cfg", "req"),
        P(),
        P(),
        P(),
        P(),
        P(("blk", "req"), None),
        P(),
        P(("blk", "req"), None),
        P(("blk", "req"), None),
        P(("blk", "req"), None),
        P(),
        P(("blk", "req"), None),
        P(),
        P(),
    )
    body = fused if fits(mesh) else local
    return jax.shard_map(
        body, mesh=mesh, in_specs=placed, out_specs=P("cfg", ("blk", "req")), check_vma=False
    )
```

```python
import math

import jax
import jax.numpy as jnp
from jax import lax
from jax.experimental import pallas as pl
from jax.experimental.pallas import tpu as pltpu
from jax.sharding import PartitionSpec as P

H = 16
HD = 128
FF = 5632
TOPK = 2


EPS = 1e-05


def joined(shard, axis, combine):
    everything = jax.tree.map(
        lambda part, kind: lax.all_gather(part.astype(kind), axis),
        shard,
        (jnp.bfloat16, jnp.bfloat16, jnp.bfloat16),
    )

    def take(k):
        return jax.tree.map(lambda part, own: part[k].astype(own.dtype), everything, shard)

    return lax.fori_loop(
        1, lax.axis_size(axis), lambda k, so_far: combine(so_far, take(k)), take(0)
    )


def swapped(value, axis, bit):
    mask = 2**bit
    pairs = [(source, source ^ mask) for source in range(lax.axis_size(axis))]
    return lax.ppermute(value, axis, pairs)


def rms_scale(values):
    return values * lax.rsqrt(jnp.mean(values * values, axis=-1, keepdims=True) + EPS)


def pair_gates(logits, chosen_ids):
    experts = jnp.arange(logits.shape[-1])
    picked = jnp.sum(
        jnp.where(chosen_ids[:, :, None] == experts[None, None, :], logits[:, None, :], 0.0),
        axis=-1,
    )
    first = jax.nn.sigmoid(picked[:, 0] - picked[:, 1])
    second = jax.nn.sigmoid(picked[:, 1] - picked[:, 0])
    return jnp.stack([first, second], axis=1)


def merge_parts(first_part, second_part):
    top_first, sum_first, acc_first = first_part
    top_second, sum_second, acc_second = second_part
    highest = jnp.maximum(top_first, top_second)
    scale_first = jnp.exp(top_first - highest)
    scale_second = jnp.exp(top_second - highest)
    merged_sum = sum_first * scale_first + sum_second * scale_second
    merged_acc = acc_first * scale_first[..., None] + acc_second * scale_second[..., None]
    return (highest, merged_sum, merged_acc)


def local(
    residual,
    queries,
    new_entries,
    key_cache,
    value_cache,
    lengths,
    attention_ids,
    expert_ids,
    attention_router,
    expert_router,
    attention_output,
    expert_gain,
    expert_gate,
    expert_up,
    expert_down,
    final_gain,
    unembedding,
    tenant_sizes,
    guidance,
):
    factor_scale = 1.0 / math.sqrt(HD)
    slot_rows = queries.shape[1]
    positions_local = key_cache.shape[2]
    feature_width = H * HD
    blk_index = lax.axis_index("blk")
    linear_index = blk_index * lax.axis_size("req") + lax.axis_index("req")
    query_heads = queries[0].reshape(slot_rows, TOPK, H, HD)
    key_heads = key_cache[0].reshape(slot_rows, positions_local, H, HD)
    value_heads = value_cache[0].reshape(slot_rows, positions_local, H, HD)
    scores = (
        jnp.einsum("rkhd,rphd->rkhp", query_heads, key_heads, preferred_element_type=jnp.float32)
        * factor_scale
    )
    positions = blk_index * positions_local + jnp.arange(positions_local)
    live = (positions[None, :] < lengths[0][:, None])[:, None, None, :]
    local_top = jnp.max(jnp.where(live, scores, -1e30), axis=-1)
    weights_local = jnp.where(live, jnp.exp(scores - local_top[..., None]), 0.0)
    weight_sums = jnp.sum(weights_local, axis=-1)
    weighted = jnp.einsum(
        "rkhp,rphd->rkhd",
        weights_local.astype(jnp.bfloat16),
        value_heads,
        preferred_element_type=jnp.float32,
    )
    highest, weight_sums, weighted = joined((local_top, weight_sums, weighted), "blk", merge_parts)
    new_keys = new_entries[0][:, 0].reshape(slot_rows, H, HD)
    new_values = new_entries[0][:, 1].reshape(slot_rows, H, HD)
    new_score = (
        jnp.einsum("rkhd,rhd->rkh", query_heads, new_keys, preferred_element_type=jnp.float32)
        * factor_scale
    )
    peak = jnp.maximum(highest, new_score)
    shrink = jnp.exp(highest - peak)
    fresh = jnp.exp(new_score - peak)
    denominator = weight_sums * shrink + fresh
    fresh_rounded = fresh.astype(jnp.bfloat16)
    numerator = weighted * shrink[..., None] + jnp.einsum(
        "rkh,rhd->rkhd", fresh_rounded, new_values, preferred_element_type=jnp.float32
    )
    attention_out = (
        (numerator / denominator[..., None])
        .astype(jnp.bfloat16)
        .reshape(slot_rows, TOPK, feature_width)
    )
    inputs = residual[0].astype(jnp.float32)
    normed_input = rms_scale(inputs).astype(jnp.bfloat16)
    attention_gates = pair_gates(
        jnp.dot(normed_input, attention_router, preferred_element_type=jnp.float32), attention_ids
    )
    proj_rows = attention_output.shape[0]
    first_row = linear_index * proj_rows
    own_expert = first_row // feature_width
    own_column = first_row % feature_width
    picked = (attention_ids == own_expert).astype(jnp.float32) * attention_gates
    columns = lax.dynamic_slice_in_dim(
        lax.all_gather(attention_out, "req", axis=0, tiled=True), own_column, proj_rows, 2
    ).astype(jnp.float32)
    selected = jnp.sum(picked[:, :, None] * columns, axis=1).astype(jnp.bfloat16)
    proj_terms = jnp.dot(selected, attention_output, preferred_element_type=jnp.float32)
    attention_proj = lax.psum(proj_terms, ("blk", "req"))
    middle = inputs + attention_proj
    expert_input = (rms_scale(middle) * expert_gain.astype(jnp.float32)).astype(jnp.bfloat16)
    expert_gates = pair_gates(
        jnp.dot(expert_input, expert_router, preferred_element_type=jnp.float32), expert_ids
    )
    hidden_rows = expert_gate.shape[0]
    hidden_expert = linear_index * hidden_rows // FF
    expert_share = jnp.sum((expert_ids == hidden_expert).astype(jnp.float32) * expert_gates, axis=1)
    gate_values = jnp.einsum(
        "rd,fd->rf", expert_input, expert_gate, preferred_element_type=jnp.float32
    )
    up_values = jnp.einsum("rd,fd->rf", expert_input, expert_up, preferred_element_type=jnp.float32)
    expert_hidden = (jax.nn.silu(gate_values) * up_values * expert_share[:, None]).astype(
        jnp.bfloat16
    )
    expert_terms = jnp.dot(expert_hidden, expert_down, preferred_element_type=jnp.float32)
    expert_out = lax.psum(expert_terms, ("blk", "req"))
    final_input = (rms_scale(middle + expert_out) * final_gain.astype(jnp.float32)).astype(
        jnp.bfloat16
    )
    logits = jnp.einsum("rd,vd->rv", final_input, unembedding, preferred_element_type=jnp.float32)
    stream_index = lax.axis_index("cfg")
    half_rows = logits.shape[0] // 2
    own_rows = lax.dynamic_slice_in_dim(logits, stream_index * half_rows, half_rows, 0)
    other_rows = lax.dynamic_slice_in_dim(logits, (1 - stream_index) * half_rows, half_rows, 0)
    partner = swapped(other_rows, "cfg", 0)
    first_stream = stream_index == 0
    conditional = jnp.where(first_stream, own_rows, partner)
    unconditional = jnp.where(first_stream, partner, own_rows)
    request_index = stream_index * half_rows + jnp.arange(half_rows)
    tenant_ends = jnp.cumsum(tenant_sizes)
    tenant = jnp.sum((request_index[:, None] >= tenant_ends[None, :]).astype(jnp.int32), axis=1)
    tenant_onehot = tenant[:, None] == jnp.arange(tenant_sizes.shape[0])[None, :]
    factor = (
        jnp.sum(jnp.where(tenant_onehot, guidance[None, :], 0), axis=1).astype(jnp.float32) / 4.0
    )
    return unconditional + factor[:, None] * (conditional - unconditional)


LANES = 128
F32 = jnp.float32
BF16 = jnp.bfloat16
MESH = pl.DeviceIdType.MESH
DEAD = -1e30


def fits(mesh):
    shape = dict(mesh.shape)
    return shape["cfg"] == 2 and shape["blk"] == 4 and shape["req"] == 4


def dot_nt(left, right):
    return lax.dot_general(left, right, (((1,), (1,)), ((), ())), preferred_element_type=F32)


def gates_of(logits, ids):
    experts = lax.broadcasted_iota(jnp.int32, logits.shape, 0)
    first = jnp.sum(jnp.where(experts == ids[0:1], logits, 0.0), axis=0, keepdims=True)
    second = jnp.sum(jnp.where(experts == ids[1:2], logits, 0.0), axis=0, keepdims=True)
    return jax.nn.sigmoid(first - second), jax.nn.sigmoid(second - first)


def expert_share_of(logits, ids, expert):
    first, second = gates_of(logits, ids)
    return jnp.where(ids[0:1] == expert, first, 0.0) + jnp.where(ids[1:2] == expert, second, 0.0)


def as_column(row):
    extent = row.shape[1]
    diagonal = lax.broadcasted_iota(jnp.int32, (extent, extent), 0) == lax.broadcasted_iota(
        jnp.int32, (extent, extent), 1
    )
    return jnp.sum(jnp.where(diagonal, row, 0.0), axis=1, keepdims=True)


def as_row(column):
    extent = column.shape[0]
    diagonal = lax.broadcasted_iota(jnp.int32, (extent, extent), 0) == lax.broadcasted_iota(
        jnp.int32, (extent, extent), 1
    )
    return jnp.sum(jnp.where(diagonal, column, 0.0), axis=0, keepdims=True)


def step_kernel(
    n_blk,
    n_req,
    residual,
    queries,
    new_entries,
    key_cache,
    value_cache,
    lengths,
    att_ids,
    exp_ids,
    att_router,
    exp_router,
    w_proj,
    gain_in,
    gain_out,
    w_gate,
    w_up,
    w_down,
    w_head,
    sizes,
    guidance,
    out,
    keys,
    values,
    v_proj,
    v_gate,
    v_up,
    v_down,
    v_head,
    send_a,
    recv_a,
    joint,
    send_r,
    recv_r,
    send_g,
    recv_g,
    send_q,
    recv_q,
    send_f,
    recv_f,
    own_middle,
    kv_sem,
    w_sem,
    sems_s,
    sems_r,
    sems_a,
    sems_g,
    gain_rows,
    send_l,
    recv_l,
    swap_sem,
):
    n = n_blk * n_req
    cfg = lax.axis_index("cfg")
    blk = lax.axis_index("blk")
    req = lax.axis_index("req")
    me = blk * n_req + req
    rows = queries.shape[1]
    local_pos = key_cache.shape[2]
    width = H * HD

    barrier = pltpu.get_barrier_semaphore()

    def greet(k, carry):
        other = lax.rem(me + k, n)
        for side in (0, 1):
            pl.semaphore_signal(
                barrier,
                inc=1,
                device_id=(side, other // n_req, lax.rem(other, n_req)),
                device_id_type=MESH,
            )
        return carry

    lax.fori_loop(1, n, greet, 0)
    pl.semaphore_signal(barrier, inc=1, device_id=(1 - cfg, blk, req), device_id_type=MESH)

    cache_copies = []
    for r in range(rows):
        for which, (source, target) in enumerate(((key_cache, keys), (value_cache, values))):
            copy = pltpu.make_async_copy(
                source.at[0, r], target.at[r, pl.ds(0, local_pos)], kv_sem.at[which, r]
            )
            copy.start()
            cache_copies.append(copy)
    weight_copies = []
    for source, target in (
        (w_proj, v_proj),
        (w_gate, v_gate),
        (w_up, v_up),
        (w_down, v_down),
        (w_head, v_head),
    ):
        extent = target.shape[0]
        own_first = cfg * (source.shape[0] - extent)
        sem = w_sem.at[len(weight_copies)]
        for first in range(0, extent, 512):
            size = min(512, extent - first)
            pltpu.make_async_copy(
                source.at[pl.ds(pl.multiple_of(own_first + first, 16), size)],
                target.at[pl.ds(first, size)],
                sem,
            ).start()
        weight_copies.append(
            pltpu.make_async_copy(source.at[pl.ds(0, extent)], target, sem)
        )

    upper = blk // 2
    near = (blk, 4 * upper + 1 - blk, 2 - upper, 3 - 3 * upper)
    columns = n_req * LANES

    def send_plane(source_of, target, plane, own, phase, recv_sem_of):
        for away in (0, 1):
            side = 1 - cfg if away else cfg

            def go(k, carry, away=away, side=side):
                to = lax.rem(req + k, n_req)
                pltpu.make_async_remote_copy(
                    src_ref=source_of(side, plane * n_req + to),
                    dst_ref=target.at[cfg, me],
                    send_sem=sems_s.at[phase, away],
                    recv_sem=recv_sem_of(away),
                    device_id=(side, plane, to),
                    device_id_type=MESH,
                ).start()
                return carry

            lax.fori_loop(1 if own and away == 0 else 0, n_req, go, 0, unroll=True)

    def wait_plane(target, count, sem):
        blocks = target.at[0, pl.ds(0, count)]
        pltpu.make_async_remote_copy(
            src_ref=blocks,
            dst_ref=blocks,
            send_sem=sem,
            recv_sem=sem,
            device_id=(1 - cfg, blk, req),
            device_id_type=MESH,
        ).wait_recv()

    def wait_sent(target, phase):
        for away in (0, 1):
            blocks = target.at[0, pl.ds(0, n - 1 + away)]
            pltpu.make_async_remote_copy(
                src_ref=blocks,
                dst_ref=blocks,
                send_sem=sems_s.at[phase, away],
                recv_sem=sems_s.at[phase, away],
                device_id=(1 - cfg, blk, req),
                device_id_type=MESH,
            ).wait_send()

    def plane_of(buf, plane):
        return jnp.concatenate(
            [
                jnp.concatenate(
                    [buf[stream, plane * n_req + j].astype(F32) for j in range(n_req)], axis=1
                )
                for stream in (0, 1)
            ],
            axis=0,
        )

    def gain_of(buf, plane):
        return jnp.concatenate(
            [buf[pl.ds(plane * n_req + j, 1), :] for j in range(n_req)], axis=1
        )

    def columns_of(plane):
        return pl.ds(pl.multiple_of(plane * columns, columns), columns)

    extra = keys.shape[1] - local_pos
    head_of_row = lax.rem(lax.broadcasted_iota(jnp.int32, (TOPK * H, 1), 0), H)
    head_of_column = lax.broadcasted_iota(jnp.int32, (TOPK * H, width), 1) // HD
    own_head = head_of_row == head_of_column
    place = lax.broadcasted_iota(jnp.int32, (1, keys.shape[1]), 1)
    new_row = lax.broadcasted_iota(jnp.int32, (extra, 1), 0) == 0
    query_all = queries[0].astype(F32)
    inputs = residual[0].astype(F32)
    normed = rms_scale(inputs).astype(BF16)
    ids_here = att_ids[...]
    chosen = (H, ids_here.shape[1])
    mine = lax.broadcasted_iota(jnp.int32, chosen, 1) == (
        req * rows + lax.broadcasted_iota(jnp.int32, chosen, 0) // (H // rows)
    )
    gate_columns = [
        jnp.sum(jnp.where(mine, gate, 0.0), axis=1, keepdims=True)
        for gate in gates_of(dot_nt(att_router[...], normed), ids_here)
    ]
    id_columns = [
        jnp.sum(jnp.where(mine, ids_here[k : k + 1], 0), axis=1, keepdims=True)
        for k in range(TOPK)
    ]
    outs = []
    tops = []
    for copy in cache_copies:
        copy.wait()
    for r in range(rows):
        entries = new_entries[0, r].astype(F32)
        keys[r, pl.ds(local_pos, extra)] = jnp.where(new_row, entries[0:1], 0.0).astype(BF16)
        values[r, pl.ds(local_pos, extra)] = jnp.where(new_row, entries[1:2], 0.0).astype(BF16)
        spread = jnp.concatenate(
            [
                jnp.broadcast_to(query_all[r : r + 1, k * width : (k + 1) * width], (H, width))
                for k in range(TOPK)
            ],
            axis=0,
        )
        spread = jnp.where(own_head, spread, 0.0).astype(BF16)
        scores = dot_nt(spread, keys[r]) * (1.0 / math.sqrt(HD))
        cached = (place < local_pos) & (place + blk * local_pos < lengths[0, r])
        live = cached | ((place == local_pos) & (blk == 0))
        top = jnp.max(jnp.where(live, scores, DEAD), axis=1, keepdims=True)
        weights = jnp.where(live, jnp.exp(scores - top), 0.0)
        total = jnp.sum(weights, axis=1, keepdims=True)
        wide = jnp.dot(weights.astype(BF16), values[r], preferred_element_type=F32)
        acc = jnp.zeros((TOPK * H, HD), F32)
        for h in range(H):
            acc = acc + jnp.where(head_of_row == h, wide[:, h * HD : (h + 1) * HD], 0.0)
        alive = total > 0.0
        safe = jnp.where(alive, total, 1.0)
        outs.append(acc / safe)
        tops.append(jnp.where(alive, top + jnp.log(safe), DEAD))

    quarter = H // 4
    lane = lax.broadcasted_iota(jnp.int32, (H, LANES), 1)
    for part in range(4):
        cuts = [slice(k * H + part * quarter, k * H + (part + 1) * quarter) for k in range(TOPK)]
        blocks = [jnp.concatenate([each[cut] for each in outs], axis=0) for cut in cuts]
        levels = [jnp.concatenate([each[cut] for each in tops], axis=0) for cut in cuts]
        for e in range(n // 2):
            first = id_columns[0] == e
            second = id_columns[1] == e
            block = jnp.where(first, gate_columns[0] * blocks[0], 0.0) + jnp.where(
                second, gate_columns[1] * blocks[1], 0.0
            )
            level = jnp.where(first, levels[0], jnp.where(second, levels[1], 0.0))
            high = level.astype(BF16).astype(F32)
            mid = (level - high).astype(BF16).astype(F32)
            stats = jnp.where(
                lane == 0,
                high,
                jnp.where(lane == 1, mid, jnp.where(lane == 2, level - high - mid, 0.0)),
            )
            send_a[part % 2, 2 * e + part // 2] = jnp.concatenate(
                [block, stats], axis=0
            ).astype(BF16)

    spot = (n - n_req, 2 * H, LANES)
    empty = (lax.broadcasted_iota(jnp.int32, spot, 1) >= H) & (
        lax.broadcasted_iota(jnp.int32, spot, 2) == 0
    )
    recv_a[1, pl.ds(n_req, n - n_req)] = jnp.where(empty, DEAD, 0.0).astype(BF16)
    pl.semaphore_wait(barrier, 2 * n - 1)

    @pl.when(cfg * blk == 0)
    def _():
        for step in range(n_blk):
            send_plane(
                lambda side, other: send_a.at[side, other],
                recv_a,
                near[n_blk - 1 - step],
                step == n_blk - 1,
                0,
                lambda away: sems_a.at[cfg],
            )

    recv_a[cfg, me] = send_a[cfg, me]
    gain_rows[0] = gain_in[...].astype(F32)
    gain_rows[1] = gain_out[...].astype(F32)
    weight_copies[0].wait()

    @pl.when(cfg == 0)
    def _():
        wait_plane(recv_a, n - 1, sems_a.at[0])
        wait_plane(recv_a, n_req, sems_a.at[1])

    @pl.when(cfg == 1)
    def _():
        wait_plane(recv_a, n, sems_a.at[0])

    @pl.when(cfg * (blk + 1) == 1)
    def _():
        wait_plane(recv_a, n_req - 1, sems_a.at[1])

    @pl.when(cfg * blk > 0)
    def _():
        wait_plane(recv_a, n_req, sems_a.at[1])

    for stream in (0, 1):
        for q in range(n_req):
            blocks = []
            levels = []
            for b in range(n_blk):
                message = recv_a[stream, b * n_req + q].astype(F32)
                levels.append(jnp.sum(message[H:], axis=1, keepdims=True))
                blocks.append(message[:H])
            peak = levels[0]
            for b in range(1, n_blk):
                peak = jnp.maximum(peak, levels[b])
            total = jnp.zeros_like(peak)
            mixed = jnp.zeros_like(blocks[0])
            for b in range(n_blk):
                weight = jnp.exp(levels[b] - peak)
                total = total + weight
                mixed = mixed + weight * blocks[b]
            joint[pl.ds((stream * n_req + q) * H, H)] = mixed / total
    gathered = jnp.concatenate(
        [joint[pl.ds(h, 2 * n_req * rows, stride=quarter), :] for h in range(quarter)], axis=1
    )
    selected = gathered.astype(BF16)

    def scatter(left, weights, send_buf, target, phase):
        for step in range(n_blk):
            plane = near[n_blk - 1 - step]
            part = jnp.dot(left, weights[:, columns_of(plane)], preferred_element_type=F32)
            for stream in (0, 1):
                for j in range(n_req):
                    send_buf[stream, plane * n_req + j] = part[
                        stream * H : (stream + 1) * H, j * LANES : (j + 1) * LANES
                    ].astype(BF16)
            send_plane(
                lambda side, other: send_buf.at[side, other],
                target,
                plane,
                step == n_blk - 1,
                phase,
                lambda away: sems_r.at[phase, away],
            )
        target[cfg, me] = send_buf[cfg, me]
        wait_plane(target, n - 1, sems_r.at[phase, 0])
        wait_plane(target, n, sems_r.at[phase, 1])

    def summed(buf):
        total = 0.0
        for stream in (0, 1):
            for k in range(n):
                total = total + buf[stream, k].astype(F32)
        return total

    def gather(block, target, phase):
        for step in range(n_blk):
            send_plane(
                lambda side, other: block,
                target,
                near[n_blk - 1 - step],
                step == n_blk - 1,
                phase,
                lambda away: sems_g.at[phase, away, blk],
            )
        target[cfg, me] = block[...]

    def gathered_plane(step, target, phase):
        plane = near[step]
        wait_plane(target, n_req - 1 if step == 0 else n_req, sems_g.at[phase, 0, plane])
        wait_plane(target, n_req, sems_g.at[phase, 1, plane])
        return plane, plane_of(target, plane)

    def squares(values):
        return jnp.sum(values * values, axis=1, keepdims=True)

    scatter(selected, v_proj, send_r, recv_r, 1)
    own_column = pl.multiple_of(me * LANES, LANES)
    own_middle[...] = summed(recv_r) + residual[0, :, pl.ds(own_column, LANES)].astype(F32)
    send_g[...] = own_middle[...].astype(BF16)
    gather(send_g, recv_g, 2)
    weight_copies[1].wait()
    weight_copies[2].wait()
    square_sum = 0.0
    gate_sum = 0.0
    up_sum = 0.0
    router_sum = 0.0
    for step in range(n_blk):
        plane, part = gathered_plane(step, recv_g, 2)
        square_sum = square_sum + squares(part)
        part = (part * gain_of(gain_rows.at[0], plane)).astype(BF16)
        gate_sum = gate_sum + dot_nt(part, v_gate[:, columns_of(plane)])
        up_sum = up_sum + dot_nt(part, v_up[:, columns_of(plane)])
        router_sum = router_sum + dot_nt(exp_router[:, columns_of(plane)], part)
    scale = lax.rsqrt(square_sum / (n * LANES) + EPS)
    share = as_column(
        expert_share_of(
            router_sum * as_row(scale),
            jnp.concatenate([exp_ids[...]] * 2, axis=1),
            2 * me * v_gate.shape[0] // FF,
        )
    )
    all_hidden = (jax.nn.silu(gate_sum * scale) * (up_sum * (scale * share))).astype(BF16)
    weight_copies[3].wait()
    scatter(all_hidden, v_down, send_q, recv_q, 3)
    send_f[...] = (own_middle[...] + summed(recv_q)).astype(BF16)
    gather(send_f, recv_f, 4)
    weight_copies[4].wait()

    guided_rows = out.shape[0]
    request = lax.broadcasted_iota(jnp.int32, (2 * guided_rows, LANES), 0)
    tenant = jnp.zeros_like(request)
    end = 0
    for t in range(sizes.shape[0]):
        end = end + sizes[t]
        tenant = tenant + jnp.where(request >= end, 1, 0)
    guide = jnp.zeros_like(request)
    for t in range(sizes.shape[0]):
        guide = guide + jnp.where(tenant == t, guidance[t], 0)
    factor = guide.astype(F32)[:, 0:1] / 4.0
    square_sum = 0.0
    logits = 0.0
    for step in range(n_blk):
        plane, part = gathered_plane(step, recv_f, 4)
        square_sum = square_sum + squares(part)
        part = (part * gain_of(gain_rows.at[1], plane)).astype(BF16)
        logits = logits + dot_nt(part, v_head[:, columns_of(plane)])
    logits = logits * lax.rsqrt(square_sum / (n * LANES) + EPS)
    conditional, unconditional = logits[:H], logits[H:]
    guided = unconditional + factor * (conditional - unconditional)
    lower, upper = guided[:guided_rows], guided[guided_rows:]
    send_l[...] = jnp.where(cfg == 0, upper, lower)
    swap = pltpu.make_async_remote_copy(
        src_ref=send_l,
        dst_ref=recv_l,
        send_sem=swap_sem.at[0],
        recv_sem=swap_sem.at[1],
        device_id=(1 - cfg, blk, req),
        device_id_type=MESH,
    )
    swap.start()

    @pl.when(cfg * blk == 0)
    def _():
        wait_sent(recv_a, 0)

    for phase, target in ((1, recv_r), (2, recv_g), (3, recv_q), (4, recv_f)):
        wait_sent(target, phase)
    held = jnp.where(cfg == 0, lower, upper)
    swap.wait()
    other_words = recv_l[...]
    words = v_head.shape[0]
    out[:, :words] = jnp.where(cfg == 0, held, other_words)
    out[:, words:] = jnp.where(cfg == 0, other_words, held)[:, 2 * words - out.shape[1] :]


def fused(
    residual,
    queries,
    new_entries,
    key_cache,
    value_cache,
    lengths,
    attention_ids,
    expert_ids,
    attention_router,
    expert_router,
    attention_output,
    expert_gain,
    expert_gate,
    expert_up,
    expert_down,
    final_gain,
    unembedding,
    tenant_sizes,
    guidance,
):
    n_blk, n_req = lax.axis_size("blk"), lax.axis_size("req")
    n = n_blk * n_req
    requests = residual.shape[1]
    rows = queries.shape[1]
    positions = key_cache.shape[2] + 16
    width = H * HD
    D = residual.shape[2]
    head_words = (unembedding.shape[0] // 2 + LANES - 1) // LANES * LANES
    vmem = pl.BlockSpec(memory_space=pltpu.VMEM)
    smem = pl.BlockSpec(memory_space=pltpu.SMEM)
    hbm = pl.BlockSpec(memory_space=pl.ANY)
    block = (requests, LANES)
    weights = attention_output.size + 3 * expert_gate.size + unembedding.size
    return pl.pallas_call(
        lambda *refs: step_kernel(n_blk, n_req, *refs),
        out_shape=jax.ShapeDtypeStruct((requests // 2, unembedding.shape[0]), F32),
        in_specs=[
            vmem, vmem, vmem, hbm, hbm, smem, vmem, vmem, vmem, vmem,
            hbm, vmem, vmem, hbm, hbm, hbm, hbm, smem, smem,
        ],
        out_specs=vmem,
        scratch_shapes=[
            pltpu.VMEM((rows, positions, width), BF16),
            pltpu.VMEM((rows, positions, width), BF16),
            pltpu.VMEM((attention_output.shape[0] // 2, D), BF16),
            pltpu.VMEM((expert_gate.shape[0] // 2, D), BF16),
            pltpu.VMEM((expert_gate.shape[0] // 2, D), BF16),
            pltpu.VMEM((expert_gate.shape[0] // 2, D), BF16),
            pltpu.VMEM((head_words, D), BF16),
            pltpu.VMEM((2, n, 2 * H, LANES), BF16),
            pltpu.VMEM((2, n, 2 * H, LANES), BF16),
            pltpu.VMEM((2 * requests * H // 4, LANES), F32),
            pltpu.VMEM((2, n, *block), BF16),
            pltpu.VMEM((2, n, *block), BF16),
            pltpu.VMEM(block, BF16),
            pltpu.VMEM((2, n, *block), BF16),
            pltpu.VMEM((2, n, *block), BF16),
            pltpu.VMEM((2, n, *block), BF16),
            pltpu.VMEM(block, BF16),
            pltpu.VMEM((2, n, *block), BF16),
            pltpu.VMEM(block, F32),
            pltpu.SemaphoreType.DMA((2, rows)),
            pltpu.SemaphoreType.DMA((5,)),
            pltpu.SemaphoreType.DMA((5, 2)),
            pltpu.SemaphoreType.DMA((5, 2)),
            pltpu.SemaphoreType.DMA((2,)),
            pltpu.SemaphoreType.DMA((5, 2, n_blk)),
            pltpu.VMEM((2, n, LANES), F32),
            pltpu.VMEM((requests // 2, head_words), F32),
            pltpu.VMEM((requests // 2, head_words), F32),
            pltpu.SemaphoreType.DMA((2,)),
        ],
        compiler_params=pltpu.CompilerParams(
            collective_id=0, has_side_effects=True, vmem_limit_bytes=60 * 2**20
        ),
        cost_estimate=pl.CostEstimate(
            flops=2 * requests * weights, bytes_accessed=2 * weights, transcendentals=0
        ),
    )(
        residual,
        queries,
        new_entries,
        key_cache,
        value_cache,
        lengths,
        attention_ids.T,
        expert_ids.T,
        attention_router.T,
        expert_router.T,
        attention_output,
        expert_gain.reshape(n, LANES),
        final_gain.reshape(n, LANES),
        expert_gate,
        expert_up,
        expert_down,
        unembedding,
        tenant_sizes,
        guidance,
    )


def solution(mesh):
    placed = (
        P("cfg", None, None),
        P("cfg", "req", None),
        P("cfg", "req", None, None),
        P("cfg", "req", "blk", None),
        P("cfg", "req", "blk", None),
        P("cfg", "req"),
        P(),
        P(),
        P(),
        P(),
        P(("blk", "req"), None),
        P(),
        P(("blk", "req"), None),
        P(("blk", "req"), None),
        P(("blk", "req"), None),
        P(),
        P(("blk", "req"), None),
        P(),
        P(),
    )
    body = fused if fits(mesh) else local
    return jax.shard_map(
        body, mesh=mesh, in_specs=placed, out_specs=P("cfg", ("blk", "req")), check_vma=False
    )
```

```python
import math

import jax
import jax.numpy as jnp
from jax import lax
from jax.experimental import pallas as pl
from jax.experimental.pallas import tpu as pltpu
from jax.sharding import PartitionSpec as P

H = 16
HD = 128
FF = 5632
TOPK = 2


EPS = 1e-05


def joined(shard, axis, combine):
    everything = jax.tree.map(
        lambda part, kind: lax.all_gather(part.astype(kind), axis),
        shard,
        (jnp.bfloat16, jnp.bfloat16, jnp.bfloat16),
    )

    def take(k):
        return jax.tree.map(lambda part, own: part[k].astype(own.dtype), everything, shard)

    return lax.fori_loop(
        1, lax.axis_size(axis), lambda k, so_far: combine(so_far, take(k)), take(0)
    )


def swapped(value, axis, bit):
    mask = 2**bit
    pairs = [(source, source ^ mask) for source in range(lax.axis_size(axis))]
    return lax.ppermute(value, axis, pairs)


def rms_scale(values):
    return values * lax.rsqrt(jnp.mean(values * values, axis=-1, keepdims=True) + EPS)


def pair_gates(logits, chosen_ids):
    experts = jnp.arange(logits.shape[-1])
    picked = jnp.sum(
        jnp.where(chosen_ids[:, :, None] == experts[None, None, :], logits[:, None, :], 0.0),
        axis=-1,
    )
    first = jax.nn.sigmoid(picked[:, 0] - picked[:, 1])
    second = jax.nn.sigmoid(picked[:, 1] - picked[:, 0])
    return jnp.stack([first, second], axis=1)


def merge_parts(first_part, second_part):
    top_first, sum_first, acc_first = first_part
    top_second, sum_second, acc_second = second_part
    highest = jnp.maximum(top_first, top_second)
    scale_first = jnp.exp(top_first - highest)
    scale_second = jnp.exp(top_second - highest)
    merged_sum = sum_first * scale_first + sum_second * scale_second
    merged_acc = acc_first * scale_first[..., None] + acc_second * scale_second[..., None]
    return (highest, merged_sum, merged_acc)


def local(
    residual,
    queries,
    new_entries,
    key_cache,
    value_cache,
    lengths,
    attention_ids,
    expert_ids,
    attention_router,
    expert_router,
    attention_output,
    expert_gain,
    expert_gate,
    expert_up,
    expert_down,
    final_gain,
    unembedding,
    tenant_sizes,
    guidance,
):
    factor_scale = 1.0 / math.sqrt(HD)
    slot_rows = queries.shape[1]
    positions_local = key_cache.shape[2]
    feature_width = H * HD
    blk_index = lax.axis_index("blk")
    linear_index = blk_index * lax.axis_size("req") + lax.axis_index("req")
    query_heads = queries[0].reshape(slot_rows, TOPK, H, HD)
    key_heads = key_cache[0].reshape(slot_rows, positions_local, H, HD)
    value_heads = value_cache[0].reshape(slot_rows, positions_local, H, HD)
    scores = (
        jnp.einsum("rkhd,rphd->rkhp", query_heads, key_heads, preferred_element_type=jnp.float32)
        * factor_scale
    )
    positions = blk_index * positions_local + jnp.arange(positions_local)
    live = (positions[None, :] < lengths[0][:, None])[:, None, None, :]
    local_top = jnp.max(jnp.where(live, scores, -1e30), axis=-1)
    weights_local = jnp.where(live, jnp.exp(scores - local_top[..., None]), 0.0)
    weight_sums = jnp.sum(weights_local, axis=-1)
    weighted = jnp.einsum(
        "rkhp,rphd->rkhd",
        weights_local.astype(jnp.bfloat16),
        value_heads,
        preferred_element_type=jnp.float32,
    )
    highest, weight_sums, weighted = joined((local_top, weight_sums, weighted), "blk", merge_parts)
    new_keys = new_entries[0][:, 0].reshape(slot_rows, H, HD)
    new_values = new_entries[0][:, 1].reshape(slot_rows, H, HD)
    new_score = (
        jnp.einsum("rkhd,rhd->rkh", query_heads, new_keys, preferred_element_type=jnp.float32)
        * factor_scale
    )
    peak = jnp.maximum(highest, new_score)
    shrink = jnp.exp(highest - peak)
    fresh = jnp.exp(new_score - peak)
    denominator = weight_sums * shrink + fresh
    fresh_rounded = fresh.astype(jnp.bfloat16)
    numerator = weighted * shrink[..., None] + jnp.einsum(
        "rkh,rhd->rkhd", fresh_rounded, new_values, preferred_element_type=jnp.float32
    )
    attention_out = (
        (numerator / denominator[..., None])
        .astype(jnp.bfloat16)
        .reshape(slot_rows, TOPK, feature_width)
    )
    inputs = residual[0].astype(jnp.float32)
    normed_input = rms_scale(inputs).astype(jnp.bfloat16)
    attention_gates = pair_gates(
        jnp.dot(normed_input, attention_router, preferred_element_type=jnp.float32), attention_ids
    )
    proj_rows = attention_output.shape[0]
    first_row = linear_index * proj_rows
    own_expert = first_row // feature_width
    own_column = first_row % feature_width
    picked = (attention_ids == own_expert).astype(jnp.float32) * attention_gates
    columns = lax.dynamic_slice_in_dim(
        lax.all_gather(attention_out, "req", axis=0, tiled=True), own_column, proj_rows, 2
    ).astype(jnp.float32)
    selected = jnp.sum(picked[:, :, None] * columns, axis=1).astype(jnp.bfloat16)
    proj_terms = jnp.dot(selected, attention_output, preferred_element_type=jnp.float32)
    attention_proj = lax.psum(proj_terms, ("blk", "req"))
    middle = inputs + attention_proj
    expert_input = (rms_scale(middle) * expert_gain.astype(jnp.float32)).astype(jnp.bfloat16)
    expert_gates = pair_gates(
        jnp.dot(expert_input, expert_router, preferred_element_type=jnp.float32), expert_ids
    )
    hidden_rows = expert_gate.shape[0]
    hidden_expert = linear_index * hidden_rows // FF
    expert_share = jnp.sum((expert_ids == hidden_expert).astype(jnp.float32) * expert_gates, axis=1)
    gate_values = jnp.einsum(
        "rd,fd->rf", expert_input, expert_gate, preferred_element_type=jnp.float32
    )
    up_values = jnp.einsum("rd,fd->rf", expert_input, expert_up, preferred_element_type=jnp.float32)
    expert_hidden = (jax.nn.silu(gate_values) * up_values * expert_share[:, None]).astype(
        jnp.bfloat16
    )
    expert_terms = jnp.dot(expert_hidden, expert_down, preferred_element_type=jnp.float32)
    expert_out = lax.psum(expert_terms, ("blk", "req"))
    final_input = (rms_scale(middle + expert_out) * final_gain.astype(jnp.float32)).astype(
        jnp.bfloat16
    )
    logits = jnp.einsum("rd,vd->rv", final_input, unembedding, preferred_element_type=jnp.float32)
    stream_index = lax.axis_index("cfg")
    half_rows = logits.shape[0] // 2
    own_rows = lax.dynamic_slice_in_dim(logits, stream_index * half_rows, half_rows, 0)
    other_rows = lax.dynamic_slice_in_dim(logits, (1 - stream_index) * half_rows, half_rows, 0)
    partner = swapped(other_rows, "cfg", 0)
    first_stream = stream_index == 0
    conditional = jnp.where(first_stream, own_rows, partner)
    unconditional = jnp.where(first_stream, partner, own_rows)
    request_index = stream_index * half_rows + jnp.arange(half_rows)
    tenant_ends = jnp.cumsum(tenant_sizes)
    tenant = jnp.sum((request_index[:, None] >= tenant_ends[None, :]).astype(jnp.int32), axis=1)
    tenant_onehot = tenant[:, None] == jnp.arange(tenant_sizes.shape[0])[None, :]
    factor = (
        jnp.sum(jnp.where(tenant_onehot, guidance[None, :], 0), axis=1).astype(jnp.float32) / 4.0
    )
    return unconditional + factor[:, None] * (conditional - unconditional)


LANES = 128
F32 = jnp.float32
BF16 = jnp.bfloat16
MESH = pl.DeviceIdType.MESH
DEAD = -1e30


def fits(mesh):
    shape = dict(mesh.shape)
    return shape["cfg"] == 2 and shape["blk"] == 4 and shape["req"] == 4


def dot_nt(left, right):
    return lax.dot_general(left, right, (((1,), (1,)), ((), ())), preferred_element_type=F32)


def gates_of(logits, ids):
    experts = lax.broadcasted_iota(jnp.int32, logits.shape, 0)
    first = jnp.sum(jnp.where(experts == ids[0:1], logits, 0.0), axis=0, keepdims=True)
    second = jnp.sum(jnp.where(experts == ids[1:2], logits, 0.0), axis=0, keepdims=True)
    return jax.nn.sigmoid(first - second), jax.nn.sigmoid(second - first)


def expert_share_of(logits, ids, expert):
    first, second = gates_of(logits, ids)
    return jnp.where(ids[0:1] == expert, first, 0.0) + jnp.where(ids[1:2] == expert, second, 0.0)


def as_column(row):
    extent = row.shape[1]
    diagonal = lax.broadcasted_iota(jnp.int32, (extent, extent), 0) == lax.broadcasted_iota(
        jnp.int32, (extent, extent), 1
    )
    return jnp.sum(jnp.where(diagonal, row, 0.0), axis=1, keepdims=True)


def as_row(column):
    extent = column.shape[0]
    diagonal = lax.broadcasted_iota(jnp.int32, (extent, extent), 0) == lax.broadcasted_iota(
        jnp.int32, (extent, extent), 1
    )
    return jnp.sum(jnp.where(diagonal, column, 0.0), axis=0, keepdims=True)


def step_kernel(
    n_blk,
    n_req,
    residual,
    queries,
    new_entries,
    key_cache,
    value_cache,
    lengths,
    att_ids,
    exp_ids,
    att_router,
    exp_router,
    w_proj,
    gain_in,
    gain_out,
    w_gate,
    w_up,
    w_down,
    w_head,
    sizes,
    guidance,
    out,
    keys,
    values,
    v_proj,
    v_gate,
    v_up,
    v_down,
    v_head,
    send_a,
    recv_a,
    joint,
    send_r,
    recv_r,
    send_g,
    recv_g,
    send_q,
    recv_q,
    send_f,
    recv_f,
    own_middle,
    kv_sem,
    w_sem,
    sems_s,
    sems_r,
    sems_a,
    sems_g,
    gain_rows,
    send_l,
    recv_l,
    swap_sem,
):
    n = n_blk * n_req
    cfg = lax.axis_index("cfg")
    blk = lax.axis_index("blk")
    req = lax.axis_index("req")
    me = blk * n_req + req
    rows = queries.shape[1]
    local_pos = key_cache.shape[2]
    width = H * HD

    barrier = pltpu.get_barrier_semaphore()

    cache_copies = []
    for r in range(rows):
        for which, (source, target) in enumerate(((key_cache, keys), (value_cache, values))):
            copy = pltpu.make_async_copy(
                source.at[0, r], target.at[r, pl.ds(0, local_pos)], kv_sem.at[which, r]
            )
            copy.start()
            cache_copies.append(copy)
    weight_copies = []
    for source, target in (
        (w_proj, v_proj),
        (w_gate, v_gate),
        (w_up, v_up),
        (w_down, v_down),
        (w_head, v_head),
    ):
        extent = target.shape[0]
        own_first = cfg * (source.shape[0] - extent)
        sem = w_sem.at[len(weight_copies)]
        for first in range(0, extent, 512):
            size = min(512, extent - first)
            pltpu.make_async_copy(
                source.at[pl.ds(pl.multiple_of(own_first + first, 16), size)],
                target.at[pl.ds(first, size)],
                sem,
            ).start()
        weight_copies.append(
            pltpu.make_async_copy(source.at[pl.ds(0, extent)], target, sem)
        )

    def greet(k, carry):
        other = lax.rem(me + k, n)
        for side in (0, 1):
            pl.semaphore_signal(
                barrier,
                inc=1,
                device_id=(side, other // n_req, lax.rem(other, n_req)),
                device_id_type=MESH,
            )
        return carry

    lax.fori_loop(1, n, greet, 0, unroll=True)
    pl.semaphore_signal(barrier, inc=1, device_id=(1 - cfg, blk, req), device_id_type=MESH)

    upper = blk // 2
    near = (blk, 4 * upper + 1 - blk, 2 - upper, 3 - 3 * upper)
    columns = n_req * LANES

    def send_plane(source_of, target, plane, own, phase, recv_sem_of):
        for away in (0, 1):
            side = 1 - cfg if away else cfg

            def go(k, carry, away=away, side=side):
                to = lax.rem(req + k, n_req)
                pltpu.make_async_remote_copy(
                    src_ref=source_of(side, plane * n_req + to),
                    dst_ref=target.at[cfg, me],
                    send_sem=sems_s.at[phase, away],
                    recv_sem=recv_sem_of(away),
                    device_id=(side, plane, to),
                    device_id_type=MESH,
                ).start()
                return carry

            lax.fori_loop(1 if own and away == 0 else 0, n_req, go, 0, unroll=True)

    def wait_plane(target, count, sem):
        blocks = target.at[0, pl.ds(0, count)]
        pltpu.make_async_remote_copy(
            src_ref=blocks,
            dst_ref=blocks,
            send_sem=sem,
            recv_sem=sem,
            device_id=(1 - cfg, blk, req),
            device_id_type=MESH,
        ).wait_recv()

    def wait_sent(target, phase):
        for away in (0, 1):
            blocks = target.at[0, pl.ds(0, n - 1 + away)]
            pltpu.make_async_remote_copy(
                src_ref=blocks,
                dst_ref=blocks,
                send_sem=sems_s.at[phase, away],
                recv_sem=sems_s.at[phase, away],
                device_id=(1 - cfg, blk, req),
                device_id_type=MESH,
            ).wait_send()

    def plane_of(buf, plane):
        return jnp.concatenate(
            [
                jnp.concatenate(
                    [buf[stream, plane * n_req + j].astype(F32) for j in range(n_req)], axis=1
                )
                for stream in (0, 1)
            ],
            axis=0,
        )

    def gain_of(buf, plane):
        return jnp.concatenate(
            [buf[pl.ds(plane * n_req + j, 1), :] for j in range(n_req)], axis=1
        )

    def columns_of(plane):
        return pl.ds(pl.multiple_of(plane * columns, columns), columns)

    extra = keys.shape[1] - local_pos
    head_of_row = lax.rem(lax.broadcasted_iota(jnp.int32, (TOPK * H, 1), 0), H)
    head_of_column = lax.broadcasted_iota(jnp.int32, (TOPK * H, width), 1) // HD
    own_head = head_of_row == head_of_column
    place = lax.broadcasted_iota(jnp.int32, (1, keys.shape[1]), 1)
    new_row = lax.broadcasted_iota(jnp.int32, (extra, 1), 0) == 0
    query_all = queries[0].astype(F32)
    inputs = residual[0].astype(F32)
    normed = rms_scale(inputs).astype(BF16)
    ids_here = att_ids[...]
    chosen = (H, ids_here.shape[1])
    mine = lax.broadcasted_iota(jnp.int32, chosen, 1) == (
        req * rows + lax.broadcasted_iota(jnp.int32, chosen, 0) // (H // rows)
    )
    gate_columns = [
        jnp.sum(jnp.where(mine, gate, 0.0), axis=1, keepdims=True)
        for gate in gates_of(dot_nt(att_router[...], normed), ids_here)
    ]
    id_columns = [
        jnp.sum(jnp.where(mine, ids_here[k : k + 1], 0), axis=1, keepdims=True)
        for k in range(TOPK)
    ]
    outs = []
    tops = []
    for copy in cache_copies:
        copy.wait()
    for r in range(rows):
        entries = new_entries[0, r].astype(F32)
        keys[r, pl.ds(local_pos, extra)] = jnp.where(new_row, entries[0:1], 0.0).astype(BF16)
        values[r, pl.ds(local_pos, extra)] = jnp.where(new_row, entries[1:2], 0.0).astype(BF16)
        spread = jnp.concatenate(
            [
                jnp.broadcast_to(query_all[r : r + 1, k * width : (k + 1) * width], (H, width))
                for k in range(TOPK)
            ],
            axis=0,
        )
        spread = jnp.where(own_head, spread, 0.0).astype(BF16)
        scores = dot_nt(spread, keys[r]) * (1.0 / math.sqrt(HD))
        cached = (place < local_pos) & (place + blk * local_pos < lengths[0, r])
        live = cached | ((place == local_pos) & (blk == 0))
        top = jnp.max(jnp.where(live, scores, DEAD), axis=1, keepdims=True)
        weights = jnp.where(live, jnp.exp(scores - top), 0.0)
        total = jnp.sum(weights, axis=1, keepdims=True)
        wide = jnp.dot(weights.astype(BF16), values[r], preferred_element_type=F32)
        acc = jnp.zeros((TOPK * H, HD), F32)
        for h in range(H):
            acc = acc + jnp.where(head_of_row == h, wide[:, h * HD : (h + 1) * HD], 0.0)
        alive = total > 0.0
        safe = jnp.where(alive, total, 1.0)
        outs.append(acc / safe)
        tops.append(jnp.where(alive, top + jnp.log(safe), DEAD))

    quarter = H // 4
    lane = lax.broadcasted_iota(jnp.int32, (H, LANES), 1)
    for part in range(4):
        cuts = [slice(k * H + part * quarter, k * H + (part + 1) * quarter) for k in range(TOPK)]
        blocks = [jnp.concatenate([each[cut] for each in outs], axis=0) for cut in cuts]
        levels = [jnp.concatenate([each[cut] for each in tops], axis=0) for cut in cuts]
        for e in range(n // 2):
            first = id_columns[0] == e
            second = id_columns[1] == e
            block = jnp.where(first, gate_columns[0] * blocks[0], 0.0) + jnp.where(
                second, gate_columns[1] * blocks[1], 0.0
            )
            level = jnp.where(first, levels[0], jnp.where(second, levels[1], 0.0))
            high = level.astype(BF16).astype(F32)
            mid = (level - high).astype(BF16).astype(F32)
            stats = jnp.where(
                lane == 0,
                high,
                jnp.where(lane == 1, mid, jnp.where(lane == 2, level - high - mid, 0.0)),
            )
            send_a[part % 2, 2 * e + part // 2] = jnp.concatenate(
                [block, stats], axis=0
            ).astype(BF16)

    pl.semaphore_wait(barrier, 2 * n - 1)

    @pl.when(cfg * blk == 0)
    def _():
        for step in range(n_blk):
            send_plane(
                lambda side, other: send_a.at[side, other],
                recv_a,
                near[n_blk - 1 - step],
                step == n_blk - 1,
                0,
                lambda away: sems_a.at[cfg],
            )

    recv_a[cfg, me] = send_a[cfg, me]
    gain_rows[0] = gain_in[...].astype(F32)
    gain_rows[1] = gain_out[...].astype(F32)
    weight_copies[0].wait()

    @pl.when(cfg == 0)
    def _():
        wait_plane(recv_a, n - 1, sems_a.at[0])
        wait_plane(recv_a, n_req, sems_a.at[1])

    @pl.when(cfg == 1)
    def _():
        wait_plane(recv_a, n, sems_a.at[0])

    @pl.when(cfg * (blk + 1) == 1)
    def _():
        wait_plane(recv_a, n_req - 1, sems_a.at[1])

    @pl.when(cfg * blk > 0)
    def _():
        wait_plane(recv_a, n_req, sems_a.at[1])

    for q in range(n_req):
        blocks = []
        levels = []
        for b in range(n_blk):
            message = recv_a[0, b * n_req + q].astype(F32)
            levels.append(jnp.sum(message[H:], axis=1, keepdims=True))
            blocks.append(message[:H])
        peak = levels[0]
        for b in range(1, n_blk):
            peak = jnp.maximum(peak, levels[b])
        total = jnp.zeros_like(peak)
        mixed = jnp.zeros_like(blocks[0])
        for b in range(n_blk):
            weight = jnp.exp(levels[b] - peak)
            total = total + weight
            mixed = mixed + weight * blocks[b]
        joint[pl.ds(q * H, H)] = mixed / total
        joint[pl.ds((n_req + q) * H, H)] = recv_a[1, q, pl.ds(0, H)].astype(F32)
    gathered = jnp.concatenate(
        [joint[pl.ds(h, 2 * n_req * rows, stride=quarter), :] for h in range(quarter)], axis=1
    )
    selected = gathered.astype(BF16)

    def scatter(left, weights, send_buf, target, phase):
        for step in range(n_blk):
            plane = near[n_blk - 1 - step]
            part = jnp.dot(left, weights[:, columns_of(plane)], preferred_element_type=F32)
            for stream in (0, 1):
                for j in range(n_req):
                    send_buf[stream, plane * n_req + j] = part[
                        stream * H : (stream + 1) * H, j * LANES : (j + 1) * LANES
                    ].astype(BF16)
            send_plane(
                lambda side, other: send_buf.at[side, other],
                target,
                plane,
                step == n_blk - 1,
                phase,
                lambda away: sems_r.at[phase, away],
            )
        target[cfg, me] = send_buf[cfg, me]
        wait_plane(target, n - 1, sems_r.at[phase, 0])
        wait_plane(target, n, sems_r.at[phase, 1])

    def summed(buf):
        total = 0.0
        for stream in (0, 1):
            for k in range(n):
                total = total + buf[stream, k].astype(F32)
        return total

    def gather(block, target, phase):
        for step in range(n_blk):
            send_plane(
                lambda side, other: block,
                target,
                near[n_blk - 1 - step],
                step == n_blk - 1,
                phase,
                lambda away: sems_g.at[phase, away, blk],
            )
        target[cfg, me] = block[...]

    def gathered_plane(step, target, phase):
        plane = near[step]
        wait_plane(target, n_req - 1 if step == 0 else n_req, sems_g.at[phase, 0, plane])
        wait_plane(target, n_req, sems_g.at[phase, 1, plane])
        return plane, plane_of(target, plane)

    def squares(values):
        return jnp.sum(values * values, axis=1, keepdims=True)

    scatter(selected, v_proj, send_r, recv_r, 1)
    own_column = pl.multiple_of(me * LANES, LANES)
    own_middle[...] = summed(recv_r) + residual[0, :, pl.ds(own_column, LANES)].astype(F32)
    send_g[...] = own_middle[...].astype(BF16)
    gather(send_g, recv_g, 2)
    weight_copies[1].wait()
    weight_copies[2].wait()
    square_sum = 0.0
    gate_sum = 0.0
    up_sum = 0.0
    router_sum = 0.0
    for step in range(n_blk):
        plane, part = gathered_plane(step, recv_g, 2)
        square_sum = square_sum + squares(part)
        part = (part * gain_of(gain_rows.at[0], plane)).astype(BF16)
        gate_sum = gate_sum + dot_nt(part, v_gate[:, columns_of(plane)])
        up_sum = up_sum + dot_nt(part, v_up[:, columns_of(plane)])
        router_sum = router_sum + dot_nt(exp_router[:, columns_of(plane)], part)
    scale = lax.rsqrt(square_sum / (n * LANES) + EPS)
    share = as_column(
        expert_share_of(
            router_sum * as_row(scale),
            jnp.concatenate([exp_ids[...]] * 2, axis=1),
            2 * me * v_gate.shape[0] // FF,
        )
    )
    all_hidden = (jax.nn.silu(gate_sum * scale) * (up_sum * (scale * share))).astype(BF16)
    weight_copies[3].wait()
    scatter(all_hidden, v_down, send_q, recv_q, 3)
    send_f[...] = (own_middle[...] + summed(recv_q)).astype(BF16)
    gather(send_f, recv_f, 4)
    weight_copies[4].wait()

    guided_rows = out.shape[0]
    request = lax.broadcasted_iota(jnp.int32, (2 * guided_rows, LANES), 0)
    tenant = jnp.zeros_like(request)
    end = 0
    for t in range(sizes.shape[0]):
        end = end + sizes[t]
        tenant = tenant + jnp.where(request >= end, 1, 0)
    guide = jnp.zeros_like(request)
    for t in range(sizes.shape[0]):
        guide = guide + jnp.where(tenant == t, guidance[t], 0)
    factor = guide.astype(F32)[:, 0:1] / 4.0
    square_sum = 0.0
    logits = 0.0
    for step in range(n_blk):
        plane, part = gathered_plane(step, recv_f, 4)
        square_sum = square_sum + squares(part)
        part = (part * gain_of(gain_rows.at[1], plane)).astype(BF16)
        logits = logits + dot_nt(part, v_head[:, columns_of(plane)])
    logits = logits * lax.rsqrt(square_sum / (n * LANES) + EPS)
    conditional, unconditional = logits[:H], logits[H:]
    guided = unconditional + factor * (conditional - unconditional)
    lower, upper = guided[:guided_rows], guided[guided_rows:]
    send_l[...] = jnp.where(cfg == 0, upper, lower)
    swap = pltpu.make_async_remote_copy(
        src_ref=send_l,
        dst_ref=recv_l,
        send_sem=swap_sem.at[0],
        recv_sem=swap_sem.at[1],
        device_id=(1 - cfg, blk, req),
        device_id_type=MESH,
    )
    swap.start()

    @pl.when(cfg * blk == 0)
    def _():
        wait_sent(recv_a, 0)

    for phase, target in ((1, recv_r), (2, recv_g), (3, recv_q), (4, recv_f)):
        wait_sent(target, phase)
    held = jnp.where(cfg == 0, lower, upper)
    swap.wait()
    other_words = recv_l[...]
    words = v_head.shape[0]
    out[:, :words] = jnp.where(cfg == 0, held, other_words)
    out[:, words:] = jnp.where(cfg == 0, other_words, held)[:, 2 * words - out.shape[1] :]


def fused(
    residual,
    queries,
    new_entries,
    key_cache,
    value_cache,
    lengths,
    attention_ids,
    expert_ids,
    attention_router,
    expert_router,
    attention_output,
    expert_gain,
    expert_gate,
    expert_up,
    expert_down,
    final_gain,
    unembedding,
    tenant_sizes,
    guidance,
):
    n_blk, n_req = lax.axis_size("blk"), lax.axis_size("req")
    n = n_blk * n_req
    requests = residual.shape[1]
    rows = queries.shape[1]
    positions = key_cache.shape[2] + 16
    width = H * HD
    D = residual.shape[2]
    head_words = (unembedding.shape[0] // 2 + LANES - 1) // LANES * LANES
    vmem = pl.BlockSpec(memory_space=pltpu.VMEM)
    smem = pl.BlockSpec(memory_space=pltpu.SMEM)
    hbm = pl.BlockSpec(memory_space=pl.ANY)
    block = (requests, LANES)
    weights = attention_output.size + 3 * expert_gate.size + unembedding.size
    return pl.pallas_call(
        lambda *refs: step_kernel(n_blk, n_req, *refs),
        out_shape=jax.ShapeDtypeStruct((requests // 2, unembedding.shape[0]), F32),
        in_specs=[
            vmem, vmem, vmem, hbm, hbm, smem, vmem, vmem, vmem, vmem,
            hbm, vmem, vmem, hbm, hbm, hbm, hbm, smem, smem,
        ],
        out_specs=vmem,
        scratch_shapes=[
            pltpu.VMEM((rows, positions, width), BF16),
            pltpu.VMEM((rows, positions, width), BF16),
            pltpu.VMEM((attention_output.shape[0] // 2, D), BF16),
            pltpu.VMEM((expert_gate.shape[0] // 2, D), BF16),
            pltpu.VMEM((expert_gate.shape[0] // 2, D), BF16),
            pltpu.VMEM((expert_gate.shape[0] // 2, D), BF16),
            pltpu.VMEM((head_words, D), BF16),
            pltpu.VMEM((2, n, 2 * H, LANES), BF16),
            pltpu.VMEM((2, n, 2 * H, LANES), BF16),
            pltpu.VMEM((2 * requests * H // 4, LANES), F32),
            pltpu.VMEM((2, n, *block), BF16),
            pltpu.VMEM((2, n, *block), BF16),
            pltpu.VMEM(block, BF16),
            pltpu.VMEM((2, n, *block), BF16),
            pltpu.VMEM((2, n, *block), BF16),
            pltpu.VMEM((2, n, *block), BF16),
            pltpu.VMEM(block, BF16),
            pltpu.VMEM((2, n, *block), BF16),
            pltpu.VMEM(block, F32),
            pltpu.SemaphoreType.DMA((2, rows)),
            pltpu.SemaphoreType.DMA((5,)),
            pltpu.SemaphoreType.DMA((5, 2)),
            pltpu.SemaphoreType.DMA((5, 2)),
            pltpu.SemaphoreType.DMA((2,)),
            pltpu.SemaphoreType.DMA((5, 2, n_blk)),
            pltpu.VMEM((2, n, LANES), F32),
            pltpu.VMEM((requests // 2, head_words), F32),
            pltpu.VMEM((requests // 2, head_words), F32),
            pltpu.SemaphoreType.DMA((2,)),
        ],
        compiler_params=pltpu.CompilerParams(
            collective_id=0, has_side_effects=True, vmem_limit_bytes=60 * 2**20
        ),
        cost_estimate=pl.CostEstimate(
            flops=2 * requests * weights, bytes_accessed=2 * weights, transcendentals=0
        ),
    )(
        residual,
        queries,
        new_entries,
        key_cache,
        value_cache,
        lengths,
        attention_ids.T,
        expert_ids.T,
        attention_router.T,
        expert_router.T,
        attention_output,
        expert_gain.reshape(n, LANES),
        final_gain.reshape(n, LANES),
        expert_gate,
        expert_up,
        expert_down,
        unembedding,
        tenant_sizes,
        guidance,
    )


def solution(mesh):
    placed = (
        P("cfg", None, None),
        P("cfg", "req", None),
        P("cfg", "req", None, None),
        P("cfg", "req", "blk", None),
        P("cfg", "req", "blk", None),
        P("cfg", "req"),
        P(),
        P(),
        P(),
        P(),
        P(("blk", "req"), None),
        P(),
        P(("blk", "req"), None),
        P(("blk", "req"), None),
        P(("blk", "req"), None),
        P(),
        P(("blk", "req"), None),
        P(),
        P(),
    )
    body = fused if fits(mesh) else local
    return jax.shard_map(
        body, mesh=mesh, in_specs=placed, out_specs=P("cfg", ("blk", "req")), check_vma=False
    )
```
